32 devices in a mesh: dp: 8 (over z, x), own: 4 (over y, core).
Axes of the slice: x: 2, y: 2, z: 4, core: 2. Of those that a mesh axis runs over, the one named last changes fastest.
Arguments:
- grads: bfloat16 [8, 4, 1024, 1024], P('dp', 'own'), may hold values from -6 to 6
- left: float32 [4, 1024, 1024], P('own', 'dp')
- right: float32 [4, 1024, 1024], P('own', 'dp')
- root_left: bfloat16 [4, 1024, 1024], P('own', 'dp'), as said below
- root_right: bfloat16 [4, 1024, 1024], P('own', 'dp')
- first: float32 [4, 1024, 1024], P('own', 'dp'), may hold values from -1.1 to 1.1
- second: float32 [4, 1024, 1024], P('own', 'dp'), may hold values from 0.003 to 0.05
- owner: int32 [4], replicated, may hold values from 0 to 3, each once
Outputs:
- new_left: float32 [4, 1024, 1024], P('own', 'dp')
- new_right: float32 [4, 1024, 1024], P('own', 'dp')
- new_first: float32 [4, 1024, 1024], P('own', 'dp')
- new_second: float32 [4, 1024, 1024], P('own', 'dp')
- direction: bfloat16 [4, 1024, 1024], P(None, 'dp')
The draws below stay inside these ranges and needn't reach their ends.
Inputs may be any that keep to these rules, and one draw needn't show every extreme that they name: owner is a permutation of 0 to 3. root_left and root_right are symmetric.
All inputs are finite; a program needn't handle non-finite values.
Results may differ from the reference program's by a relative error of at most 0.015.
Values may be sent and summed in bfloat16 or wider, within the bound.
A program may use at most 64 MiB of HBM per device.

```python
import math
import jax
import jax.numpy as jnp
from jax import lax

B = 1024
NB = 4
N_DP = 8


def symmetric_block(key, diag_lo, diag_hi, spread):
    noise_key, diag_key = jax.random.split(key)
    noise = jax.random.normal(noise_key, (NB, B, B), jnp.float32)
    paired = (noise + jnp.swapaxes(noise, 1, 2)) * (spread / jnp.sqrt(2.0 * B))
    diag_vals = jax.random.uniform(diag_key, (NB, B), jnp.float32, diag_lo, diag_hi)
    return paired + diag_vals[:, :, None] * jnp.eye(B, dtype=jnp.float32)[None]


def row_rise(low, factor):
    place = jnp.arange(B, dtype=jnp.float32) / (B - 1)
    return (low * jnp.exp(place * jnp.log(factor)))[None, :, None]


def draw_left(key, part):
    key = jax.random.fold_in(key, 3)
    return symmetric_block(key, 1.0, 3.0, 1.0)


def draw_right(key, part):
    key = jax.random.fold_in(key, 5)
    return symmetric_block(key, 1.0, 3.0, 1.0)


def draw_root_left(key, part):
    key = jax.random.fold_in(key, 7)
    return symmetric_block(key, 0.5, 1.5, 0.6).astype(jnp.bfloat16)


def draw_root_right(key, part):
    key = jax.random.fold_in(key, 11)
    return symmetric_block(key, 0.5, 1.5, 0.6).astype(jnp.bfloat16)


def draw_first(key, part):
    key = jax.random.fold_in(key, 13)
    values = jnp.clip(jax.random.normal(key, (NB, B, B), jnp.float32), -3.5, 3.5)
    return values * row_rise(0.03, 10.0)


def raised(result, stream_key, source, target, shards_of, factor):
    def block_of(dim):
        return (jnp.arange(result.shape[dim]) // (result.shape[dim] // shards_of)).reshape((-1,) + (1,) * (result.ndim - 1 - dim))

    first = jax.random.permutation(stream_key, shards_of)[block_of(target)]
    second = (block_of(target) + shards_of // 2) % shards_of
    return jnp.where((block_of(source) == first) | (block_of(source) == second), factor * result, result)


def level_of(stream_key, shape, shards, least, top_value):
    loudness, own = 1.0, jax.random.fold_in(stream_key, 6)
    for axis_at, shards_of in shards:
        heights = jnp.exp(jax.random.uniform(jax.random.fold_in(own, axis_at), (shards_of,), jnp.float32, least / len(shards), top_value / len(shards)))
        loudness = loudness * jnp.repeat(heights, shape[axis_at] // shards_of).reshape([-1 if axis == axis_at else 1 for axis in range(len(shape))])
    return loudness


def noise_with(key, extent, width, limit, cuts, heavy, kind=jnp.bfloat16):
    drawn = width * jax.random.normal(key, extent, jnp.float32)
    if cuts:
        drawn = drawn * level_of(key, extent, cuts, -0.22, 0.18)
    return jnp.clip(raised(drawn, jax.random.fold_in(key, 3), *heavy), -limit, limit).astype(kind)


def setup_inputs(seed: int = 0) -> dict:
    seeds = jax.random.split(jax.random.key(seed), 9)
    grads = noise_with(seeds[0], (N_DP, NB, B, B), 1.0, 6.0, ((0, 8), (1, 4)), (0, 2, 8, 2.0))
    left = draw_left(jax.random.fold_in(seeds[8], 71), 0)
    right = draw_right(jax.random.fold_in(seeds[8], 71), 0)
    root_left = draw_root_left(jax.random.fold_in(seeds[8], 71), 0)
    root_right = draw_root_right(jax.random.fold_in(seeds[8], 71), 0)
    first = draw_first(jax.random.fold_in(seeds[8], 71), 0)
    second = jnp.clip(jnp.exp(math.log(0.05) - 2.8134107 * jax.random.uniform(seeds[6], (NB, B, B), jnp.float32) ** level_of(seeds[6], (NB, B, B), ((0, 4), (1, 8)), -0.2, 0.2)), 0.003, 0.05)
    owner = jax.random.permutation(seeds[7], NB).astype(jnp.int32)
    return dict(grads=grads, left=left, right=right, root_left=root_left, root_right=root_right, first=first, second=second, owner=owner)


def reference(grads, left, right, root_left, root_right, first, second, owner):
    replicas = grads.shape[0]
    blocks = left.shape[0]

    def one(index):
        total = lax.optimization_barrier(jnp.sum(grads[:, index].astype(jnp.float32), axis=0))
        gradient = (total / replicas).astype(jnp.bfloat16)
        outer_left = lax.dot_general(gradient, gradient, (((1,), (1,)), ((), ())), preferred_element_type=jnp.float32)
        outer_right = lax.dot_general(gradient, gradient, (((0,), (0,)), ((), ())), preferred_element_type=jnp.float32)
        updated_left = 0.95 * left[index] + 0.05 * outer_left
        updated_right = 0.95 * right[index] + 0.05 * outer_right
        inner = jnp.dot(root_left[index], gradient, preferred_element_type=jnp.float32).astype(jnp.bfloat16)
        precond = jnp.dot(inner, root_right[index], preferred_element_type=jnp.float32)
        grad_value = gradient.astype(jnp.float32)
        moment_one = 0.9 * first[index] + 0.1 * grad_value
        moment_two = 0.999 * second[index] + 0.001 * grad_value * grad_value
        adam = moment_one / (jnp.sqrt(moment_two) + 1e-08)
        scale = jnp.sqrt(jnp.sum(adam * adam)) / (jnp.sqrt(jnp.sum(precond * precond)) + 1e-06)
        update = (precond * scale).astype(jnp.bfloat16)
        return (updated_left, updated_right, moment_one, moment_two, update)
    new_left, new_right, new_first, new_second, update = lax.map(one, jnp.arange(blocks, dtype=jnp.int32))
    direction = jnp.take(update, owner, axis=0)
    return (new_left, new_right, new_first, new_second, direction)
```

```python
import functools

import jax
import jax.numpy as jnp
from jax import lax
from jax.experimental import pallas as pl
from jax.experimental.pallas import tpu as pltpu
from jax.sharding import PartitionSpec as P

MESH = pl.DeviceIdType.MESH
F32 = jnp.float32
BF16 = jnp.bfloat16
LANES = 128
DEPTH = 3


def remote(src, dst, send, recv, axis, to):
    return pltpu.make_async_remote_copy(
        src_ref=src, dst_ref=dst, send_sem=send, recv_sem=recv,
        device_id={axis: to}, device_id_type=MESH,
    )


def kernel(n, owners, halves, cuts, grads, left, right, root_left, root_right, first, second, owner,
           new_left, new_right, new_first, new_second, direction,
           mine, xbuf, ubuf, dbuf, total, g, window, full, left_v, right_v, rl_v, first_v, second_v,
           inner, turned, product, parts, tile, stats, scales,
           load_sem, store_sem, xs, xr, us, ur, ds, dr, gxs, gxr, gus, gur, gds, gdr,
           rxs, rxr, rus, rur, rds, rdr, ps, pr, cs, cr, ss, sr, ts, tr):
    me = lax.axis_index("dp")
    own = lax.axis_index("own")
    size = g.shape[0]
    rows = left_v.shape[0]
    depth_z = n // 2
    z, x = me // 2, me % 2
    partner, above, below = z * 2 + 1 - x, me + 2, me - 2
    pairs = owners // 2
    pair, core = own // 2, own % 2
    part = rows // halves
    groups = size // LANES
    span = window.shape[1] // LANES
    has_above, has_below = z < depth_z - 1, z > 0

    load_mine = pltpu.make_async_copy(grads.at[:, x], mine, load_sem.at[0])
    loads = [
        pltpu.make_async_copy(src.at[0], dst, load_sem.at[i + 1])
        for i, (src, dst) in enumerate(
            ((root_left, rl_v), (first, first_v), (second, second_v), (left, left_v), (right, right_v)))
    ]
    my_rows = pl.ds(pl.multiple_of(me * rows, rows), rows)
    group = (me * rows) // LANES
    loads_rr = [
        pltpu.make_async_copy(
            root_right.at[0, :, pl.ds(pl.multiple_of(((group + k) % groups) * LANES, LANES), LANES)],
            window.at[my_rows, pl.ds(k * LANES, LANES)], load_sem.at[6 + k])
        for k in range(span)
    ]
    for copy in loads_rr:
        copy.start()
    load_mine.start()
    for copy in loads:
        copy.start()

    barrier = pltpu.get_barrier_semaphore()
    for k in range(1, n):
        pl.semaphore_signal(barrier, inc=1, device_id={"dp": (me + k) % n}, device_id_type=MESH)
    for k in range(1, owners):
        pl.semaphore_signal(barrier, inc=1, device_id={"own": (own + k) % owners}, device_id_type=MESH)
    pl.semaphore_wait(barrier, n + owners - 2)

    low = (z < depth_z // 2).astype(jnp.int32)

    def dest(s):
        if s == depth_z - 1:
            return z
        t = depth_z - 1 - s
        down_order = t - (z >= t).astype(jnp.int32)
        up_order = s + (z <= s).astype(jnp.int32)
        return low * down_order + (1 - low) * up_order

    steps = [(s, h) for s in range(depth_z) for h in range(halves)]

    def sub(h):
        return pl.ds(h * part, part)

    def send_x(i):
        s, h = steps[i]
        t = dest(s)
        return remote(grads.at[t, 1 - x, sub(h)], xbuf.at[t, sub(h)], xs.at[i], xr.at[i], "dp", partner)

    def send_up(t, h):
        return remote(mine.at[t, sub(h)], ubuf.at[t, sub(h)], us.at[t, h], ur.at[t, h], "dp", above)

    def send_down(t, h):
        return remote(mine.at[t, sub(h)], dbuf.at[t, sub(h)], ds.at[t, h], dr.at[t, h], "dp", below)

    def block(t, column, h):
        return g.at[pl.ds(pl.multiple_of((2 * t + column) * rows + h * part, part), part)]

    def gat_x(t, h):
        return remote(block(t, x, h), block(t, x, h), gxs.at[t, h], gxr.at[t, h], "dp", partner)

    def gat_up(t, h):
        return remote(block(t, x, h), block(t, x, h), gus.at[t, h], gur.at[t, h], "dp", above)

    def gat_down(t, h):
        return remote(block(t, x, h), block(t, x, h), gds.at[t, h], gdr.at[t, h], "dp", below)

    def wblock(stream, t):
        column = x if stream == 0 else 1 - x
        return window.at[pl.ds(pl.multiple_of((2 * t + column) * rows, rows), rows)]

    def root_x():
        return remote(wblock(0, z), wblock(0, z), rxs.at[0], rxr.at[0], "dp", partner)

    def root_up(stream, t):
        w = wblock(stream, t)
        return remote(w, w, rus.at[stream, t], rur.at[stream, t], "dp", above)

    def root_down(stream, t):
        w = wblock(stream, t)
        return remote(w, w, rds.at[stream, t], rdr.at[stream, t], "dp", below)

    def root_event(stream, k):
        if k == 0:
            if stream == 1:
                root_x().wait_recv()

            @pl.when(has_above)
            def _():
                root_up(stream, z).start()

            @pl.when(has_below)
            def _():
                root_down(stream, z).start()
            return

        @pl.when(z >= k)
        def _():
            root_up(stream, z - k).wait_recv()

            @pl.when(has_above)
            def _():
                root_up(stream, z - k).start()

        @pl.when(z + k < depth_z)
        def _():
            root_down(stream, z + k).wait_recv()

            @pl.when(has_below)
            def _():
                root_down(stream, z + k).start()

    for i in range(min(DEPTH, len(steps))):
        send_x(i).start()
    for copy in loads_rr:
        copy.wait()
    root_event(0, 0)
    load_mine.wait()

    events = {}
    for k in range(1, depth_z):
        events.setdefault(k - 1, []).append((0, k))
    for k in range(depth_z):
        events.setdefault(k + 1, []).append((1, k))

    for i, (s, h) in enumerate(steps):
        t = dest(s)
        send_x(i).wait_recv()
        if i + DEPTH < len(steps):
            send_x(i + DEPTH).start()
        if i == 0:
            root_x().start()
        rs = sub(h)
        acc = mine[t, rs].astype(F32) + xbuf[t, rs].astype(F32)
        if s < depth_z - 1:
            up, down = t > z, t < z

            @pl.when(up & has_below)
            def _():
                send_up(t, h).wait_recv()
                mine[t, rs] = (acc + ubuf[t, rs].astype(F32)).astype(BF16)

            @pl.when(down & has_above)
            def _():
                send_down(t, h).wait_recv()
                mine[t, rs] = (acc + dbuf[t, rs].astype(F32)).astype(BF16)

            @pl.when((up & (z == 0)) | (down & (z == depth_z - 1)))
            def _():
                mine[t, rs] = acc.astype(BF16)

            @pl.when(up)
            def _():
                send_up(t, h).start()

            @pl.when(down)
            def _():
                send_down(t, h).start()
        else:
            total[rs] = acc

            @pl.when(has_below)
            def _():
                send_up(t, h).wait_recv()
                total[rs] = total[rs] + ubuf[t, rs].astype(F32)

            @pl.when(has_above)
            def _():
                send_down(t, h).wait_recv()
                total[rs] = total[rs] + dbuf[t, rs].astype(F32)

            g[pl.ds(pl.multiple_of(me * rows + h * part, part), part)] = (total[rs] / n).astype(BF16)
            gat_x(z, h).start()

            @pl.when(has_above)
            def _():
                gat_up(z, h).start()

            @pl.when(has_below)
            def _():
                gat_down(z, h).start()
        if h == halves - 1:
            for event in events.pop(s, ()):
                root_event(*event)

    for copy in loads:
        copy.wait()
    value = g[my_rows].astype(F32)
    one = 0.9 * first_v[...] + 0.1 * value
    two = 0.999 * second_v[...] + 0.001 * value * value
    first_v[...] = one
    second_v[...] = two
    adam = one / (jnp.sqrt(two) + 1e-08)
    adam_sq = jnp.sum(jnp.sum(adam * adam, axis=0, keepdims=True), axis=1, keepdims=True)
    stores = [
        pltpu.make_async_copy(src, dst.at[0], store_sem.at[i])
        for i, (src, dst) in enumerate(
            ((first_v, new_first), (second_v, new_second), (left_v, new_left), (right_v, new_right)))
    ]
    stores[0].start()
    stores[1].start()

    for k in range(1, depth_z):
        for h in range(halves):
            @pl.when(z >= k)
            def _():
                gat_up(z - k, h).wait_recv()
                gat_x(z - k, h).start()

                @pl.when(has_above)
                def _():
                    gat_up(z - k, h).start()

            @pl.when(z + k < depth_z)
            def _():
                gat_down(z + k, h).wait_recv()
                gat_x(z + k, h).start()

                @pl.when(has_below)
                def _():
                    gat_down(z + k, h).start()
        for event in events.pop(depth_z - 1 + k, ()):
            root_event(*event)

    def rebuild(i, carry):
        r = pl.ds(pl.multiple_of(i * LANES, LANES), LANES)
        for k in range(span):
            c = pl.ds(pl.multiple_of(((i + k) % groups) * LANES, LANES), LANES)
            piece = window[r, pl.ds(k * LANES, LANES)]
            full[r, c] = piece
            if k and 2 * k < groups:
                full[c, r] = piece.T
        return carry

    lax.fori_loop(0, groups, rebuild, 0)

    for t in range(depth_z):
        for h in range(halves):
            gat_x(t, h).wait_recv()

    width = 256

    def tile_of(i):
        return pl.ds(pl.multiple_of(i * width, width), width)

    def inner_step(i, carry):
        c = tile_of(i)
        inner[:, c] = jnp.dot(rl_v[...], g[:, c], preferred_element_type=F32).astype(BF16)
        return carry

    lax.fori_loop(0, size // width, inner_step, 0)

    def parts_at(slot, cut):
        w = size // cuts
        return parts.at[slot, :, pl.ds(cut * w, w)]

    def to_pair(k, cut):
        here = parts_at(own, cut)
        return remote(here, here, ps.at[k, cut], pr.at[k, cut], "own", ((pair + k) % pairs) * 2 + core)

    def to_core(k, cut):
        here = parts_at(((pair + pairs - k) % pairs) * 2 + core, cut)
        return remote(here, here, cs.at[k, cut], cr.at[k, cut], "own", pair * 2 + 1 - core)

    precond_sq = jnp.zeros((1, 1), F32)
    for cut in range(cuts):
        w = size // cuts
        for j in range(w // width):
            c = pl.ds(cut * w + j * width, width)
            precond = jnp.dot(inner[...], full[:, c], preferred_element_type=F32)
            parts[own, :, c] = precond.astype(BF16)
            precond_sq += jnp.sum(
                jnp.sum(precond * precond, axis=0, keepdims=True), axis=1, keepdims=True)
        for k in range(1, pairs):
            to_pair(k, cut).start()
        to_core(0, cut).start()

    line = lax.broadcasted_iota(jnp.int32, tile.shape, 0)
    tile[...] = jnp.where(line == 0, adam_sq, precond_sq)
    stats[me] = tile[...]

    def norm_to(k):
        return remote(tile, stats.at[me], ss.at[k], sr.at[k], "dp", (me + k) % n)

    for k in range(1, n):
        norm_to(k).start()

    def left_step(i, carry):
        c = tile_of(i)
        outer = lax.dot_general(g[my_rows], g[c, :], (((1,), (1,)), ((), ())), preferred_element_type=F32)
        left_v[:, c] = 0.95 * left_v[:, c] + 0.05 * outer
        return carry

    lax.fori_loop(0, size // width, left_step, 0)
    stores[2].start()

    for k in range(1, n):
        norm_to(k).wait_recv()
    sums = stats[0]
    for i in range(1, n):
        sums = sums + stats[i]
    scale = jnp.sqrt(sums[0:1]) / (jnp.sqrt(sums[1:2]) + 1e-06)
    scales[own] = jnp.broadcast_to(scale, scales.shape[1:])

    def scale_to(k):
        return remote(scales.at[own], scales.at[own], ts.at[k], tr.at[k], "own", (own + k) % owners)

    for k in range(1, owners):
        scale_to(k).start()

    for cut in range(cuts):
        for k in range(1, pairs):
            to_pair(k, cut).wait_recv()
            to_core(k, cut).start()

    aligned = pl.ds(pl.multiple_of(group * LANES, LANES), LANES)

    def turn_step(i, carry):
        r = pl.ds(pl.multiple_of(i * LANES, LANES), LANES)
        turned[:, r] = g[r, aligned].T
        return carry

    lax.fori_loop(0, groups, turn_step, 0)
    offset = pl.ds(pl.multiple_of(me * rows - group * LANES, 8), rows)

    def right_step(i, carry):
        c = tile_of(i)
        product[...] = jnp.dot(turned[...], g[:, c], preferred_element_type=F32)
        right_v[:, c] = 0.95 * right_v[:, c] + 0.05 * product[offset]
        return carry

    lax.fori_loop(0, size // width, right_step, 0)
    stores[3].start()

    for k in range(1, owners):
        scale_to(k).wait_recv()
    for cut in range(cuts):
        for k in range(pairs):
            to_core(k, cut).wait_recv()
    for b in range(owners):
        direction[b] = (parts[owner[b]].astype(F32) * scales[owner[b]][0:1, 0:1]).astype(BF16)

    for i, (s, h) in enumerate(steps):
        send_x(i).wait_send()
        gat_x(s, h).wait_send()
    for t in range(depth_z):
        for h in range(halves):
            @pl.when(z < t)
            def _():
                send_up(t, h).wait_send()

            @pl.when(z > t)
            def _():
                send_down(t, h).wait_send()

            @pl.when((z >= t) & has_above)
            def _():
                gat_up(t, h).wait_send()

            @pl.when((z <= t) & has_below)
            def _():
                gat_down(t, h).wait_send()
        for stream in range(2):
            @pl.when((z >= t) & has_above)
            def _():
                root_up(stream, t).wait_send()

            @pl.when((z <= t) & has_below)
            def _():
                root_down(stream, t).wait_send()
    root_x().wait_send()
    for k in range(1, n):
        norm_to(k).wait_send()
    for k in range(1, owners):
        scale_to(k).wait_send()
    for cut in range(cuts):
        for k in range(pairs):
            to_core(k, cut).wait_send()
            if k:
                to_pair(k, cut).wait_send()
    for copy in stores:
        copy.wait()


def body(n, owners, grads, left, right, root_left, root_right, first, second, owner):
    rows, size = left.shape[1:]
    line = n // 2
    halves = max(1, rows // 64)
    cuts = 2
    pairs = owners // 2
    span = size // LANES // 2 + 1
    sem = pltpu.SemaphoreType.DMA
    stat = jax.ShapeDtypeStruct((1, rows, size), F32)
    anywhere = pl.BlockSpec(memory_space=pl.ANY)
    return pl.pallas_call(
        functools.partial(kernel, n, owners, halves, cuts),
        out_shape=(stat, stat, stat, stat, jax.ShapeDtypeStruct((owners, rows, size), BF16)),
        in_specs=[anywhere] * 7 + [pl.BlockSpec(memory_space=pltpu.SMEM)],
        out_specs=(anywhere,) * 4 + (pl.BlockSpec(memory_space=pltpu.VMEM),),
        scratch_shapes=[
            *[pltpu.VMEM((line, rows, size), BF16)] * 4,
            pltpu.VMEM((rows, size), F32),
            pltpu.VMEM((size, size), BF16),
            pltpu.VMEM((size, span * LANES), BF16),
            pltpu.VMEM((size, size), BF16),
            pltpu.VMEM((rows, size), F32),
            pltpu.VMEM((rows, size), F32),
            pltpu.VMEM((rows, size), BF16),
            pltpu.VMEM((rows, size), F32),
            pltpu.VMEM((rows, size), F32),
            pltpu.VMEM((rows, size), BF16),
            pltpu.VMEM((LANES, size), BF16),
            pltpu.VMEM((LANES, 256), F32),
            pltpu.VMEM((owners, rows, size), BF16),
            pltpu.VMEM((8, LANES), F32),
            pltpu.VMEM((n, 8, LANES), F32),
            pltpu.VMEM((owners, 8, LANES), F32),
            sem((6 + span,)), sem((4,)),
            sem((line * halves,)), sem((line * halves,)),
            *[sem((line, halves))] * 10,
            sem((1,)), sem((1,)),
            *[sem((2, line))] * 4,
            *[sem((pairs, cuts))] * 4,
            sem((n,)), sem((n,)), sem((owners,)), sem((owners,)),
        ],
        compiler_params=pltpu.CompilerParams(
            collective_id=0, has_side_effects=True, vmem_limit_bytes=40 * 1024 * 1024),
        cost_estimate=pl.CostEstimate(
            flops=8 * rows * size * size, bytes_accessed=24 * rows * size, transcendentals=rows * size),
    )(grads.reshape(line, 2, rows, size), left, right, root_left, root_right, first, second, owner)


def solution(mesh):
    split = P("own", "dp", None)
    return jax.shard_map(
        functools.partial(body, mesh.shape["dp"], mesh.shape["own"]),
        mesh=mesh,
        in_specs=(P("dp", "own", None, None),) + (split,) * 6 + (P(),),
        out_specs=(split,) * 4 + (P(None, "dp", None),),
        check_vma=False,
    )
```

```python
import functools

import jax
import jax.numpy as jnp
from jax import lax
from jax.experimental import pallas as pl
from jax.experimental.pallas import tpu as pltpu
from jax.sharding import PartitionSpec as P

MESH = pl.DeviceIdType.MESH
F32 = jnp.float32
BF16 = jnp.bfloat16
LANES = 128
DEPTH = 3


def remote(src, dst, send, recv, axis, to):
    return pltpu.make_async_remote_copy(
        src_ref=src, dst_ref=dst, send_sem=send, recv_sem=recv,
        device_id={axis: to}, device_id_type=MESH,
    )


def kernel(n, owners, halves, cuts, grads, left, right, root_left, root_right, first, second, owner,
           new_left, new_right, new_first, new_second, direction,
           mine, xbuf, ubuf, dbuf, total, g, right_rows, left_v, right_v, rl_v, first_v, second_v,
           inner, turned, product, parts, away, tile, stats, scales,
           load_sem, store_sem, xs, xr, us, ur, ds, dr, gxs, gxr, gus, gur, gds, gdr,
           rxs, rxr, rus, rur, rds, rdr, axs, axr, ps, pr, cs, cr, ss, sr, ts, tr):
    me = lax.axis_index("dp")
    own = lax.axis_index("own")
    size = g.shape[0]
    rows = left_v.shape[0]
    depth_z = n // 2
    z, x = me // 2, me % 2
    partner, above, below = z * 2 + 1 - x, me + 2, me - 2
    pairs = owners // 2
    pair, core = own // 2, own % 2
    part = rows // halves
    groups = size // LANES
    has_above, has_below = z < depth_z - 1, z > 0

    def root_rows(t):
        return right_rows.at[pl.ds(pl.multiple_of(t * rows, rows), rows)]

    load_mine = pltpu.make_async_copy(grads.at[:, x], mine, load_sem.at[0])
    loads = [
        pltpu.make_async_copy(src.at[0], dst, load_sem.at[i + 1])
        for i, (src, dst) in enumerate(
            ((root_left, rl_v.at[pl.ds(0, rows)]), (first, first_v), (second, second_v), (left, left_v), (right, right_v)))
    ]
    my_rows = pl.ds(pl.multiple_of(me * rows, rows), rows)
    group = (me * rows) // LANES
    load_rr = pltpu.make_async_copy(root_right.at[0], root_rows(z), load_sem.at[6])
    load_rr.start()
    load_mine.start()
    for copy in loads:
        copy.start()

    barrier = pltpu.get_barrier_semaphore()
    for k in range(1, n):
        pl.semaphore_signal(barrier, inc=1, device_id={"dp": (me + k) % n}, device_id_type=MESH)
    for k in range(1, owners):
        pl.semaphore_signal(barrier, inc=1, device_id={"own": (own + k) % owners}, device_id_type=MESH)
    pl.semaphore_wait(barrier, n + owners - 2)

    low = (z < depth_z // 2).astype(jnp.int32)

    def dest(s):
        if s == depth_z - 1:
            return z
        t = depth_z - 1 - s
        down_order = t - (z >= t).astype(jnp.int32)
        up_order = s + (z <= s).astype(jnp.int32)
        return low * down_order + (1 - low) * up_order

    steps = [(s, h) for s in range(depth_z) for h in range(halves)]

    def sub(h):
        return pl.ds(h * part, part)

    def send_x(i):
        s, h = steps[i]
        t = dest(s)
        return remote(grads.at[t, 1 - x, sub(h)], xbuf.at[t, sub(h)], xs.at[i], xr.at[i], "dp", partner)

    def send_up(t, h):
        return remote(mine.at[t, sub(h)], ubuf.at[t, sub(h)], us.at[t, h], ur.at[t, h], "dp", above)

    def send_down(t, h):
        return remote(mine.at[t, sub(h)], dbuf.at[t, sub(h)], ds.at[t, h], dr.at[t, h], "dp", below)

    def block(t, column, h):
        return g.at[pl.ds(pl.multiple_of((2 * t + column) * rows + h * part, part), part)]

    def gat_x(t, h):
        return remote(block(t, x, h), block(t, x, h), gxs.at[t, h], gxr.at[t, h], "dp", partner)

    def gat_up(t, h):
        return remote(block(t, x, h), block(t, x, h), gus.at[t, h], gur.at[t, h], "dp", above)

    def gat_down(t, h):
        return remote(block(t, x, h), block(t, x, h), gds.at[t, h], gdr.at[t, h], "dp", below)

    def root_x():
        return remote(rl_v.at[pl.ds(0, rows)], rl_v.at[pl.ds(rows, rows)], rxs.at[0], rxr.at[0], "dp", partner)

    def root_up(t):
        return remote(root_rows(t), root_rows(t), rus.at[t], rur.at[t], "dp", above)

    def root_down(t):
        return remote(root_rows(t), root_rows(t), rds.at[t], rdr.at[t], "dp", below)

    def root_event(k):
        if k == 0:
            @pl.when(has_above)
            def _():
                root_up(z).start()

            @pl.when(has_below)
            def _():
                root_down(z).start()
            return

        @pl.when(z >= k)
        def _():
            root_up(z - k).wait_recv()

            @pl.when(has_above)
            def _():
                root_up(z - k).start()

        @pl.when(z + k < depth_z)
        def _():
            root_down(z + k).wait_recv()

            @pl.when(has_below)
            def _():
                root_down(z + k).start()

    for i in range(min(DEPTH, len(steps))):
        send_x(i).start()
    load_rr.wait()
    root_event(0)
    load_mine.wait()

    for i, (s, h) in enumerate(steps):
        t = dest(s)
        send_x(i).wait_recv()
        if i + DEPTH < len(steps):
            send_x(i + DEPTH).start()
        if i == len(steps) - 1:
            loads[0].wait()
            root_x().start()
        rs = sub(h)
        acc = mine[t, rs].astype(F32) + xbuf[t, rs].astype(F32)
        if s < depth_z - 1:
            up, down = t > z, t < z

            @pl.when(up & has_below)
            def _():
                send_up(t, h).wait_recv()
                mine[t, rs] = (acc + ubuf[t, rs].astype(F32)).astype(BF16)

            @pl.when(down & has_above)
            def _():
                send_down(t, h).wait_recv()
                mine[t, rs] = (acc + dbuf[t, rs].astype(F32)).astype(BF16)

            @pl.when((up & (z == 0)) | (down & (z == depth_z - 1)))
            def _():
                mine[t, rs] = acc.astype(BF16)

            @pl.when(up)
            def _():
                send_up(t, h).start()

            @pl.when(down)
            def _():
                send_down(t, h).start()
        else:
            total[rs] = acc

            @pl.when(has_below)
            def _():
                send_up(t, h).wait_recv()
                total[rs] = total[rs] + ubuf[t, rs].astype(F32)

            @pl.when(has_above)
            def _():
                send_down(t, h).wait_recv()
                total[rs] = total[rs] + dbuf[t, rs].astype(F32)

            g[pl.ds(pl.multiple_of(me * rows + h * part, part), part)] = (total[rs] / n).astype(BF16)
            gat_x(z, h).start()

            @pl.when(has_above)
            def _():
                gat_up(z, h).start()

            @pl.when(has_below)
            def _():
                gat_down(z, h).start()
        if h == halves - 1 and s < depth_z - 1:
            root_event(s + 1)

    for copy in loads[1:]:
        copy.wait()
    value = g[my_rows].astype(F32)
    one = 0.9 * first_v[...] + 0.1 * value
    two = 0.999 * second_v[...] + 0.001 * value * value
    first_v[...] = one
    second_v[...] = two
    adam = one / (jnp.sqrt(two) + 1e-08)
    adam_sq = jnp.sum(jnp.sum(adam * adam, axis=0, keepdims=True), axis=1, keepdims=True)
    stores = [
        pltpu.make_async_copy(src, dst.at[0], store_sem.at[i])
        for i, (src, dst) in enumerate(
            ((first_v, new_first), (second_v, new_second), (left_v, new_left), (right_v, new_right)))
    ]
    stores[0].start()
    stores[1].start()

    width = 256
    pair_rows = 2 * rows
    stepwise = pair_rows % LANES == 0

    def tile_of(i):
        return pl.ds(pl.multiple_of(i * width, width), width)

    def absorb(t, begin):
        for h in range(halves):
            gat_x(t, h).wait_recv()
        if not stepwise:
            return
        both = pl.ds(pl.multiple_of(t * pair_rows, pair_rows), pair_rows)

        def step(i, carry):
            c = tile_of(i)
            more = jnp.dot(rl_v[:, both], g[both, c], preferred_element_type=F32)
            inner[:, c] = more if begin else inner[:, c] + more
            return carry

        lax.fori_loop(0, size // width, step, 0)

    def absorb_at(k):
        if k == 0:
            root_x().wait_recv()
            absorb(z, True)
            return

        @pl.when(z >= k)
        def _():
            absorb(z - k, False)

        @pl.when(z + k < depth_z)
        def _():
            absorb(z + k, False)

    for k in range(1, depth_z):
        for h in range(halves):
            @pl.when(z >= k)
            def _():
                gat_up(z - k, h).wait_recv()
                gat_x(z - k, h).start()

                @pl.when(has_above)
                def _():
                    gat_up(z - k, h).start()

            @pl.when(z + k < depth_z)
            def _():
                gat_down(z + k, h).wait_recv()
                gat_x(z + k, h).start()

                @pl.when(has_below)
                def _():
                    gat_down(z + k, h).start()
        absorb_at(k - 1)
    absorb_at(depth_z - 1)
    if not stepwise:
        def inner_step(i, carry):
            c = tile_of(i)
            inner[:, c] = jnp.dot(rl_v[...], g[:, c], preferred_element_type=F32)
            return carry

        lax.fori_loop(0, size // width, inner_step, 0)

    def parts_at(slot, cut):
        return parts.at[slot, x if cut == 0 else 1 - x]

    def swap():
        return remote(away, parts.at[own, x], axs.at[0], axr.at[0], "dp", partner)

    def to_pair(k, cut):
        here = parts_at(own, cut)
        return remote(here, here, ps.at[k, cut], pr.at[k, cut], "own", ((pair + k) % pairs) * 2 + core)

    def to_core(k, cut):
        here = parts_at(((pair + pairs - k) % pairs) * 2 + core, cut)
        return remote(here, here, cs.at[k, cut], cr.at[k, cut], "own", pair * 2 + 1 - core)

    precond_sq = jnp.zeros((1, 1), F32)
    rounded = inner[...].astype(BF16)
    for j in range(size // 2 // width):
        c = pl.ds(j * width, width)
        precond = lax.dot_general(
            rounded, right_rows[c, :], (((1,), (1,)), ((), ())), preferred_element_type=F32)
        parts[own, x, :, c] = precond[:rows].astype(BF16)
        away[:, c] = precond[rows:].astype(BF16)
        precond_sq += jnp.sum(
            jnp.sum(precond * precond, axis=0, keepdims=True), axis=1, keepdims=True)
    swap().start()
    for k in range(1, pairs):
        to_pair(k, 0).start()
    to_core(0, 0).start()

    line = lax.broadcasted_iota(jnp.int32, tile.shape, 0)
    tile[...] = jnp.where(line == 0, adam_sq, precond_sq)
    stats[me] = tile[...]

    def norm_to(k):
        return remote(tile, stats.at[me], ss.at[k], sr.at[k], "dp", (me + k) % n)

    for k in range(1, n):
        norm_to(k).start()

    def pass_half():
        swap().wait_recv()
        for k in range(1, pairs):
            to_pair(k, 1).start()
        to_core(0, 1).start()

    def left_step(i, carry):
        c = tile_of(i)
        outer = lax.dot_general(g[my_rows], g[c, :], (((1,), (1,)), ((), ())), preferred_element_type=F32)
        left_v[:, c] = 0.95 * left_v[:, c] + 0.05 * outer
        return carry

    lax.fori_loop(0, size // width, left_step, 0)
    stores[2].start()

    pass_half()
    for k in range(1, n):
        norm_to(k).wait_recv()
    sums = stats[0]
    for i in range(1, n):
        sums = sums + stats[i]
    scale = jnp.sqrt(sums[0:1]) / (jnp.sqrt(sums[1:2]) + 1e-06)
    scales[own] = jnp.broadcast_to(scale, scales.shape[1:])

    def scale_to(k):
        return remote(scales.at[own], scales.at[own], ts.at[k], tr.at[k], "own", (own + k) % owners)

    for k in range(1, owners):
        scale_to(k).start()

    for cut in range(cuts):
        for k in range(1, pairs):
            to_pair(k, cut).wait_recv()
            to_core(k, cut).start()

    aligned = pl.ds(pl.multiple_of(group * LANES, LANES), LANES)

    def turn_step(i, carry):
        r = pl.ds(pl.multiple_of(i * LANES, LANES), LANES)
        turned[:, r] = g[r, aligned].T
        return carry

    lax.fori_loop(0, groups, turn_step, 0)
    offset = pl.ds(pl.multiple_of(me * rows - group * LANES, 8), rows)

    def right_step(i, carry):
        c = tile_of(i)
        product[...] = jnp.dot(turned[...], g[:, c], preferred_element_type=F32)
        right_v[:, c] = 0.95 * right_v[:, c] + 0.05 * product[offset]
        return carry

    lax.fori_loop(0, size // width, right_step, 0)
    stores[3].start()

    for k in range(1, owners):
        scale_to(k).wait_recv()
    for cut in range(cuts):
        for k in range(pairs):
            to_core(k, cut).wait_recv()
    for b in range(owners):
        factor = scales[owner[b]][0:1, 0:1]
        for column in range(2):
            scaled = (parts[owner[b], column].astype(F32) * factor).astype(BF16)
            if rows % LANES:
                direction[b, :, pl.ds(column * (size // 2), size // 2)] = scaled
                continue
            for t in range(depth_z):
                direction[b, :, pl.ds((2 * t + column) * rows, rows)] = scaled[:, t * rows:(t + 1) * rows]

    for i, (s, h) in enumerate(steps):
        send_x(i).wait_send()
        gat_x(s, h).wait_send()
    for t in range(depth_z):
        for h in range(halves):
            @pl.when(z < t)
            def _():
                send_up(t, h).wait_send()

            @pl.when(z > t)
            def _():
                send_down(t, h).wait_send()

            @pl.when((z >= t) & has_above)
            def _():
                gat_up(t, h).wait_send()

            @pl.when((z <= t) & has_below)
            def _():
                gat_down(t, h).wait_send()
        @pl.when((z >= t) & has_above)
        def _():
            root_up(t).wait_send()

        @pl.when((z <= t) & has_below)
        def _():
            root_down(t).wait_send()
    root_x().wait_send()
    swap().wait_send()
    for k in range(1, n):
        norm_to(k).wait_send()
    for k in range(1, owners):
        scale_to(k).wait_send()
    for cut in range(cuts):
        for k in range(pairs):
            to_core(k, cut).wait_send()
            if k:
                to_pair(k, cut).wait_send()
    for copy in stores:
        copy.wait()


def body(n, owners, grads, left, right, root_left, root_right, first, second, owner):
    rows, size = left.shape[1:]
    line = n // 2
    halves = max(1, rows // 64)
    cuts = 2
    pairs = owners // 2
    sem = pltpu.SemaphoreType.DMA
    stat = jax.ShapeDtypeStruct((1, rows, size), F32)
    anywhere = pl.BlockSpec(memory_space=pl.ANY)
    hbm = pl.BlockSpec(memory_space=pltpu.HBM)
    *state, direction = pl.pallas_call(
        functools.partial(kernel, n, owners, halves, cuts),
        out_shape=(stat, stat, stat, stat, jax.ShapeDtypeStruct((owners, rows, size), BF16)),
        in_specs=[hbm] * 7 + [pl.BlockSpec(memory_space=pltpu.SMEM)],
        out_specs=(anywhere,) * 4 + (pl.BlockSpec(memory_space=pltpu.VMEM),),
        scratch_shapes=[
            *[pltpu.VMEM((line, rows, size), BF16)] * 4,
            pltpu.VMEM((rows, size), F32),
            pltpu.VMEM((size, size), BF16),
            pltpu.VMEM((size // 2, size), BF16),
            pltpu.VMEM((rows, size), F32),
            pltpu.VMEM((rows, size), F32),
            pltpu.VMEM((2 * rows, size), BF16),
            pltpu.VMEM((rows, size), F32),
            pltpu.VMEM((rows, size), F32),
            pltpu.VMEM((2 * rows, size), F32),
            pltpu.VMEM((LANES, size), BF16),
            pltpu.VMEM((LANES, 256), F32),
            pltpu.VMEM((owners, 2, rows, size // 2), BF16),
            pltpu.VMEM((rows, size // 2), BF16),
            pltpu.VMEM((8, LANES), F32),
            pltpu.VMEM((n, 8, LANES), F32),
            pltpu.VMEM((owners, 8, LANES), F32),
            sem((7,)), sem((4,)),
            sem((line * halves,)), sem((line * halves,)),
            *[sem((line, halves))] * 10,
            sem((1,)), sem((1,)),
            *[sem((line,))] * 4,
            sem((1,)), sem((1,)),
            *[sem((pairs, cuts))] * 4,
            sem((n,)), sem((n,)), sem((owners,)), sem((owners,)),
        ],
        compiler_params=pltpu.CompilerParams(
            collective_id=0, has_side_effects=True, vmem_limit_bytes=60 * 1024 * 1024),
        cost_estimate=pl.CostEstimate(
            flops=8 * rows * size * size, bytes_accessed=24 * rows * size, transcendentals=rows * size),
    )(grads.reshape(line, 2, rows, size), left, right, root_left, root_right, first, second, owner)
    if rows % LANES:
        direction = direction.reshape(owners, rows, 2, line, rows).swapaxes(2, 3).reshape(owners, rows, size)
    return (*state, direction)


def solution(mesh):
    split = P("own", "dp", None)
    return jax.shard_map(
        functools.partial(body, mesh.shape["dp"], mesh.shape["own"]),
        mesh=mesh,
        in_specs=(P("dp", "own", None, None),) + (split,) * 6 + (P(),),
        out_specs=(split,) * 4 + (P(None, "dp", None),),
        check_vma=False,
    )
```

```python
import functools

import jax
import jax.numpy as jnp
from jax import lax
from jax.experimental import pallas as pl
from jax.experimental.pallas import tpu as pltpu
from jax.sharding import PartitionSpec as P

MESH = pl.DeviceIdType.MESH
F32 = jnp.float32
BF16 = jnp.bfloat16
LANES = 128
DEPTH = 3
VMEM = 60 * 1024 * 1024


def remote(src, dst, send, recv, axis, to):
    return pltpu.make_async_remote_copy(
        src_ref=src, dst_ref=dst, send_sem=send, recv_sem=recv,
        device_id={axis: to}, device_id_type=MESH,
    )


def kernel(n, owners, halves, cuts, grads, left, right, root_left, root_right, first, second, owner,
           new_left, new_right, new_first, new_second, direction,
           mine, xbuf, ubuf, dbuf, total, g, right_rows, left_v, right_v, rl_v, first_v, second_v,
           inner, turned, product, parts, away, tile, stats, scales,
           load_sem, store_sem, xs, xr, us, ur, ds, dr, gxs, gxr, gus, gur, gds, gdr,
           rxs, rxr, rus, rur, rds, rdr, axs, axr, ps, pr, cs, cr, ss, sr, ts, tr):
    me = lax.axis_index("dp")
    own = lax.axis_index("own")
    size = g.shape[0]
    rows = left_v.shape[0]
    depth_z = n // 2
    z, x = me // 2, me % 2
    partner, above, below = z * 2 + 1 - x, me + 2, me - 2
    pairs = owners // 2
    pair, core = own // 2, own % 2
    part = rows // halves
    groups = size // LANES
    has_above, has_below = z < depth_z - 1, z > 0

    def root_rows(t):
        return right_rows.at[pl.ds(pl.multiple_of(t * rows, rows), rows)]

    load_mine = pltpu.make_async_copy(grads.at[:, x], mine, load_sem.at[0])
    loads = [
        pltpu.make_async_copy(src.at[0], dst, load_sem.at[i + 1])
        for i, (src, dst) in enumerate(
            ((root_left, rl_v.at[pl.ds(0, rows)]), (first, first_v), (second, second_v), (left, left_v), (right, right_v)))
    ]
    my_rows = pl.ds(pl.multiple_of(me * rows, rows), rows)
    group = (me * rows) // LANES
    load_rr = pltpu.make_async_copy(root_right.at[0], root_rows(z), load_sem.at[6])
    load_rr.start()
    load_mine.start()
    for copy in loads:
        copy.start()

    barrier = pltpu.get_barrier_semaphore()
    for k in range(1, n):
        pl.semaphore_signal(barrier, inc=1, device_id={"dp": (me + k) % n}, device_id_type=MESH)
    for k in range(1, owners):
        pl.semaphore_signal(barrier, inc=1, device_id={"own": (own + k) % owners}, device_id_type=MESH)
    pl.semaphore_wait(barrier, n + owners - 2)

    low = (z < depth_z // 2).astype(jnp.int32)

    def dest(s):
        if s == depth_z - 1:
            return z
        t = depth_z - 1 - s
        down_order = t - (z >= t).astype(jnp.int32)
        up_order = s + (z <= s).astype(jnp.int32)
        return low * down_order + (1 - low) * up_order

    steps = [(s, h) for s in range(depth_z) for h in range(halves)]

    def sub(h):
        return pl.ds(h * part, part)

    def send_x(i):
        s, h = steps[i]
        t = dest(s)
        return remote(grads.at[t, 1 - x, sub(h)], xbuf.at[t, sub(h)], xs.at[i], xr.at[i], "dp", partner)

    def send_up(t, h):
        return remote(mine.at[t, sub(h)], ubuf.at[t, sub(h)], us.at[t, h], ur.at[t, h], "dp", above)

    def send_down(t, h):
        return remote(mine.at[t, sub(h)], dbuf.at[t, sub(h)], ds.at[t, h], dr.at[t, h], "dp", below)

    def block(t, column, h):
        return g.at[pl.ds(pl.multiple_of((2 * t + column) * rows + h * part, part), part)]

    def gat_x(t, h):
        return remote(block(t, x, h), block(t, x, h), gxs.at[t, h], gxr.at[t, h], "dp", partner)

    def gat_up(t, h):
        return remote(block(t, x, h), block(t, x, h), gus.at[t, h], gur.at[t, h], "dp", above)

    def gat_down(t, h):
        return remote(block(t, x, h), block(t, x, h), gds.at[t, h], gdr.at[t, h], "dp", below)

    def root_x():
        return remote(rl_v.at[pl.ds(0, rows)], rl_v.at[pl.ds(rows, rows)], rxs.at[0], rxr.at[0], "dp", partner)

    def root_up(t):
        return remote(root_rows(t), root_rows(t), rus.at[t], rur.at[t], "dp", above)

    def root_down(t):
        return remote(root_rows(t), root_rows(t), rds.at[t], rdr.at[t], "dp", below)

    def root_event(k):
        if k == 0:
            @pl.when(has_above)
            def _():
                root_up(z).start()

            @pl.when(has_below)
            def _():
                root_down(z).start()
            return

        @pl.when(z >= k)
        def _():
            root_up(z - k).wait_recv()

            @pl.when(has_above)
            def _():
                root_up(z - k).start()

        @pl.when(z + k < depth_z)
        def _():
            root_down(z + k).wait_recv()

            @pl.when(has_below)
            def _():
                root_down(z + k).start()

    for i in range(min(DEPTH, len(steps))):
        send_x(i).start()
    load_rr.wait()
    root_event(0)
    load_mine.wait()

    for i, (s, h) in enumerate(steps):
        t = dest(s)
        send_x(i).wait_recv()
        if i + DEPTH < len(steps):
            send_x(i + DEPTH).start()
        if i == len(steps) - 1:
            loads[0].wait()
            root_x().start()
        rs = sub(h)
        acc = mine[t, rs].astype(F32) + xbuf[t, rs].astype(F32)
        if s < depth_z - 1:
            up, down = t > z, t < z

            @pl.when(up & has_below)
            def _():
                send_up(t, h).wait_recv()
                mine[t, rs] = (acc + ubuf[t, rs].astype(F32)).astype(BF16)

            @pl.when(down & has_above)
            def _():
                send_down(t, h).wait_recv()
                mine[t, rs] = (acc + dbuf[t, rs].astype(F32)).astype(BF16)

            @pl.when((up & (z == 0)) | (down & (z == depth_z - 1)))
            def _():
                mine[t, rs] = acc.astype(BF16)

            @pl.when(up)
            def _():
                send_up(t, h).start()

            @pl.when(down)
            def _():
                send_down(t, h).start()
        else:
            total[rs] = acc

            @pl.when(has_below)
            def _():
                send_up(t, h).wait_recv()
                total[rs] = total[rs] + ubuf[t, rs].astype(F32)

            @pl.when(has_above)
            def _():
                send_down(t, h).wait_recv()
                total[rs] = total[rs] + dbuf[t, rs].astype(F32)

            g[pl.ds(pl.multiple_of(me * rows + h * part, part), part)] = (total[rs] / n).astype(BF16)
            gat_x(z, h).start()

            @pl.when(has_above)
            def _():
                gat_up(z, h).start()

            @pl.when(has_below)
            def _():
                gat_down(z, h).start()
        if h == halves - 1 and 0 < s < depth_z - 1:
            root_event(s)

    for copy in loads[1:]:
        copy.wait()
    value = g[my_rows].astype(F32)
    one = 0.9 * first_v[...] + 0.1 * value
    two = 0.999 * second_v[...] + 0.001 * value * value
    first_v[...] = one
    second_v[...] = two
    adam = one / (jnp.sqrt(two) + 1e-08)
    adam_sq = jnp.sum(jnp.sum(adam * adam, axis=0, keepdims=True), axis=1, keepdims=True)
    stores = [
        pltpu.make_async_copy(src, dst.at[0], store_sem.at[i])
        for i, (src, dst) in enumerate(
            ((first_v, new_first), (second_v, new_second), (left_v, new_left), (right_v, new_right)))
    ]
    stores[0].start()
    stores[1].start()

    width = 256
    pair_rows = 2 * rows
    stepwise = pair_rows % LANES == 0

    def tile_of(i):
        return pl.ds(pl.multiple_of(i * width, width), width)

    def absorb(t, begin):
        for h in range(halves):
            gat_x(t, h).wait_recv()
        if not stepwise:
            return
        both = pl.ds(pl.multiple_of(t * pair_rows, pair_rows), pair_rows)

        def step(i, carry):
            c = tile_of(i)
            more = jnp.dot(rl_v[:, both], g[both, c], preferred_element_type=F32)
            inner[:, c] = more if begin else inner[:, c] + more
            return carry

        lax.fori_loop(0, size // width, step, 0)

    def absorb_at(k):
        if k == 0:
            root_x().wait_recv()
            absorb(z, True)
            return

        @pl.when(z >= k)
        def _():
            absorb(z - k, False)

        @pl.when(z + k < depth_z)
        def _():
            absorb(z + k, False)

    for k in range(1, depth_z):
        for h in range(halves):
            @pl.when(z >= k)
            def _():
                gat_up(z - k, h).wait_recv()
                gat_x(z - k, h).start()

                @pl.when(has_above)
                def _():
                    gat_up(z - k, h).start()

            @pl.when(z + k < depth_z)
            def _():
                gat_down(z + k, h).wait_recv()
                gat_x(z + k, h).start()

                @pl.when(has_below)
                def _():
                    gat_down(z + k, h).start()
        absorb_at(k - 1)
        if k == max(1, depth_z - 2):
            root_event(depth_z - 1)
    absorb_at(depth_z - 1)
    if not stepwise:
        def inner_step(i, carry):
            c = tile_of(i)
            inner[:, c] = jnp.dot(rl_v[...], g[:, c], preferred_element_type=F32)
            return carry

        lax.fori_loop(0, size // width, inner_step, 0)

    def parts_at(slot, cut):
        return parts.at[slot, x if cut == 0 else 1 - x]

    def swap():
        return remote(away, parts.at[own, x], axs.at[0], axr.at[0], "dp", partner)

    def to_pair(k, cut):
        here = parts_at(own, cut)
        return remote(here, here, ps.at[k, cut], pr.at[k, cut], "own", ((pair + k) % pairs) * 2 + core)

    def to_core(k, cut):
        here = parts_at(((pair + pairs - k) % pairs) * 2 + core, cut)
        return remote(here, here, cs.at[k, cut], cr.at[k, cut], "own", pair * 2 + 1 - core)

    precond_sq = jnp.zeros((1, 1), F32)
    rounded = inner[...].astype(BF16)
    for j in range(size // 2 // width):
        c = pl.ds(j * width, width)
        precond = lax.dot_general(
            rounded, right_rows[c, :], (((1,), (1,)), ((), ())), preferred_element_type=F32)
        parts[own, x, :, c] = precond[:rows].astype(BF16)
        away[:, c] = precond[rows:].astype(BF16)
        precond_sq += jnp.sum(
            jnp.sum(precond * precond, axis=0, keepdims=True), axis=1, keepdims=True)
    swap().start()
    for k in range(1, pairs):
        to_pair(k, 0).start()
    to_core(0, 0).start()

    line = lax.broadcasted_iota(jnp.int32, tile.shape, 0)
    tile[...] = jnp.where(line == 0, adam_sq, precond_sq)
    stats[me] = tile[...]

    def norm_to(k):
        return remote(tile, stats.at[me], ss.at[k], sr.at[k], "dp", (me + k) % n)

    for k in range(1, n):
        norm_to(k).start()

    def pass_half():
        swap().wait_recv()
        for k in range(1, pairs):
            to_pair(k, 1).start()
        to_core(0, 1).start()

    def left_step(i, carry):
        c = tile_of(i)
        outer = lax.dot_general(g[my_rows], g[c, :], (((1,), (1,)), ((), ())), preferred_element_type=F32)
        left_v[:, c] = 0.95 * left_v[:, c] + 0.05 * outer
        return carry

    lax.fori_loop(0, size // width, left_step, 0)
    stores[2].start()

    pass_half()
    for k in range(1, n):
        norm_to(k).wait_recv()
    sums = stats[0]
    for i in range(1, n):
        sums = sums + stats[i]
    scale = jnp.sqrt(sums[0:1]) / (jnp.sqrt(sums[1:2]) + 1e-06)
    scales[own] = jnp.broadcast_to(scale, scales.shape[1:])

    def scale_to(k):
        return remote(scales.at[own], scales.at[own], ts.at[k], tr.at[k], "own", (own + k) % owners)

    for k in range(1, owners):
        scale_to(k).start()

    for cut in range(cuts):
        for k in range(1, pairs):
            to_pair(k, cut).wait_recv()
            to_core(k, cut).start()

    aligned = pl.ds(pl.multiple_of(group * LANES, LANES), LANES)

    def turn_step(i, carry):
        r = pl.ds(pl.multiple_of(i * LANES, LANES), LANES)
        turned[:, r] = g[r, aligned].T
        return carry

    lax.fori_loop(0, groups, turn_step, 0)
    offset = pl.ds(pl.multiple_of(me * rows - group * LANES, 8), rows)

    def right_step(i, carry):
        c = tile_of(i)
        product[...] = jnp.dot(turned[...], g[:, c], preferred_element_type=F32)
        right_v[:, c] = 0.95 * right_v[:, c] + 0.05 * product[offset]
        return carry

    lax.fori_loop(0, size // width, right_step, 0)
    stores[3].start()

    for k in range(1, owners):
        scale_to(k).wait_recv()
    for cut in range(cuts):
        for k in range(pairs):
            to_core(k, cut).wait_recv()
    for b in range(owners):
        factor = scales[owner[b]][0:1, 0:1]
        for column in range(2):
            scaled = (parts[owner[b], column].astype(F32) * factor).astype(BF16)
            if rows % LANES:
                direction[b, :, pl.ds(column * (size // 2), size // 2)] = scaled
                continue
            for t in range(depth_z):
                direction[b, :, pl.ds((2 * t + column) * rows, rows)] = scaled[:, t * rows:(t + 1) * rows]

    for i, (s, h) in enumerate(steps):
        send_x(i).wait_send()
        gat_x(s, h).wait_send()
    for t in range(depth_z):
        for h in range(halves):
            @pl.when(z < t)
            def _():
                send_up(t, h).wait_send()

            @pl.when(z > t)
            def _():
                send_down(t, h).wait_send()

            @pl.when((z >= t) & has_above)
            def _():
                gat_up(t, h).wait_send()

            @pl.when((z <= t) & has_below)
            def _():
                gat_down(t, h).wait_send()
        @pl.when((z >= t) & has_above)
        def _():
            root_up(t).wait_send()

        @pl.when((z <= t) & has_below)
        def _():
            root_down(t).wait_send()
    root_x().wait_send()
    swap().wait_send()
    for k in range(1, n):
        norm_to(k).wait_send()
    for k in range(1, owners):
        scale_to(k).wait_send()
    for cut in range(cuts):
        for k in range(pairs):
            to_core(k, cut).wait_send()
            if k:
                to_pair(k, cut).wait_send()
    for copy in stores:
        copy.wait()


def finish_kernel(*refs):
    count = len(refs) // 2
    sources, targets, sem = refs[:count], refs[count:2 * count], refs[2 * count]
    copies = []
    for source, target in zip(sources, targets):
        blocks, rows, _ = source.shape
        cut = rows // 2 if blocks == 1 else rows
        for b in range(blocks):
            for at in range(0, rows, cut):
                piece = (b, pl.ds(at, cut))
                copies.append(pltpu.make_async_copy(source.at[piece], target.at[piece], sem.at[len(copies)]))
    for copy in copies:
        copy.start()
    for copy in copies:
        copy.wait()


def finish(*arrays):
    anywhere = pl.BlockSpec(memory_space=pl.ANY)
    return pl.pallas_call(
        finish_kernel,
        out_shape=tuple(jax.ShapeDtypeStruct(a.shape, a.dtype) for a in arrays),
        in_specs=[anywhere] * len(arrays),
        out_specs=(anywhere,) * len(arrays),
        scratch_shapes=[pltpu.SemaphoreType.DMA((sum(max(2, a.shape[0]) for a in arrays),))],
        compiler_params=pltpu.CompilerParams(vmem_limit_bytes=VMEM),
    )(*arrays)


def body(n, owners, grads, left, right, root_left, root_right, first, second, owner):
    rows, size = left.shape[1:]
    line = n // 2
    halves = max(1, rows // 64)
    cuts = 2
    pairs = owners // 2
    sem = pltpu.SemaphoreType.DMA
    stat = jax.ShapeDtypeStruct((1, rows, size), F32)
    anywhere = pl.BlockSpec(memory_space=pl.ANY)
    hbm = pl.BlockSpec(memory_space=pltpu.HBM)
    *state, direction = pl.pallas_call(
        functools.partial(kernel, n, owners, halves, cuts),
        out_shape=(stat, stat, stat, stat, jax.ShapeDtypeStruct((owners, rows, size), BF16)),
        in_specs=[hbm] * 7 + [pl.BlockSpec(memory_space=pltpu.SMEM)],
        out_specs=(anywhere,) * 4 + (pl.BlockSpec(memory_space=pltpu.VMEM),),
        scratch_shapes=[
            *[pltpu.VMEM((line, rows, size), BF16)] * 4,
            pltpu.VMEM((rows, size), F32),
            pltpu.VMEM((size, size), BF16),
            pltpu.VMEM((size // 2, size), BF16),
            pltpu.VMEM((rows, size), F32),
            pltpu.VMEM((rows, size), F32),
            pltpu.VMEM((2 * rows, size), BF16),
            pltpu.VMEM((rows, size), F32),
            pltpu.VMEM((rows, size), F32),
            pltpu.VMEM((2 * rows, size), F32),
            pltpu.VMEM((LANES, size), BF16),
            pltpu.VMEM((LANES, 256), F32),
            pltpu.VMEM((owners, 2, rows, size // 2), BF16),
            pltpu.VMEM((rows, size // 2), BF16),
            pltpu.VMEM((8, LANES), F32),
            pltpu.VMEM((n, 8, LANES), F32),
            pltpu.VMEM((owners, 8, LANES), F32),
            sem((7,)), sem((4,)),
            sem((line * halves,)), sem((line * halves,)),
            *[sem((line, halves))] * 10,
            sem((1,)), sem((1,)),
            *[sem((line,))] * 4,
            sem((1,)), sem((1,)),
            *[sem((pairs, cuts))] * 4,
            sem((n,)), sem((n,)), sem((owners,)), sem((owners,)),
        ],
        compiler_params=pltpu.CompilerParams(
            collective_id=0, has_side_effects=True, vmem_limit_bytes=VMEM),
        cost_estimate=pl.CostEstimate(
            flops=8 * rows * size * size, bytes_accessed=24 * rows * size, transcendentals=rows * size),
    )(grads.reshape(line, 2, rows, size), left, right, root_left, root_right, first, second, owner)
    if rows % LANES:
        direction = direction.reshape(owners, rows, 2, line, rows).swapaxes(2, 3).reshape(owners, rows, size)
    return finish(*state, direction)


def solution(mesh):
    split = P("own", "dp", None)
    return jax.shard_map(
        functools.partial(body, mesh.shape["dp"], mesh.shape["own"]),
        mesh=mesh,
        in_specs=(P("dp", "own", None, None),) + (split,) * 6 + (P(),),
        out_specs=(split,) * 4 + (P(None, "dp", None),),
        check_vma=False,
    )
```

```python
import functools

import jax
import jax.numpy as jnp
from jax import lax
from jax.experimental import pallas as pl
from jax.experimental.pallas import tpu as pltpu
from jax.sharding import PartitionSpec as P

MESH = pl.DeviceIdType.MESH
F32 = jnp.float32
BF16 = jnp.bfloat16
LANES = 128
DEPTH = 3
VMEM = 60 * 1024 * 1024


def remote(src, dst, send, recv, axis, to):
    return pltpu.make_async_remote_copy(
        src_ref=src, dst_ref=dst, send_sem=send, recv_sem=recv,
        device_id={axis: to}, device_id_type=MESH,
    )


def kernel(n, owners, halves, cuts, grads, left, right, root_left, root_right, first, second, owner,
           new_left, new_right, new_first, new_second, direction,
           mine, xbuf, ubuf, dbuf, total, g, right_rows, left_v, right_v, rl_v, first_v, second_v,
           inner, turned, product, parts, away, tile, stats, scales,
           load_sem, store_sem, xs, xr, us, ur, ds, dr, gxs, gxr, gus, gur, gds, gdr,
           rxs, rxr, rus, rur, rds, rdr, axs, axr, ps, pr, cs, cr, ss, sr, ts, tr):
    me = lax.axis_index("dp")
    own = lax.axis_index("own")
    size = g.shape[0]
    rows = left_v.shape[0]
    depth_z = n // 2
    z, x = me // 2, me % 2
    partner, above, below = z * 2 + 1 - x, me + 2, me - 2
    pairs = owners // 2
    pair, core = own // 2, own % 2
    part = rows // halves
    groups = size // LANES
    has_above, has_below = z < depth_z - 1, z > 0

    def root_rows(t):
        return right_rows.at[pl.ds(pl.multiple_of(t * rows, rows), rows)]

    load_mine = pltpu.make_async_copy(grads.at[:, x], mine, load_sem.at[0])
    loads = [
        pltpu.make_async_copy(src.at[0], dst, load_sem.at[i + 1])
        for i, (src, dst) in enumerate(
            ((root_left, rl_v.at[pl.ds(0, rows)]), (first, first_v), (second, second_v), (left, left_v), (right, right_v)))
    ]
    my_rows = pl.ds(pl.multiple_of(me * rows, rows), rows)
    group = (me * rows) // LANES
    load_rr = pltpu.make_async_copy(root_right.at[0], root_rows(z), load_sem.at[6])
    load_rr.start()
    load_mine.start()
    for copy in loads:
        copy.start()

    barrier = pltpu.get_barrier_semaphore()
    for k in range(1, n):
        pl.semaphore_signal(barrier, inc=1, device_id={"dp": (me + k) % n}, device_id_type=MESH)
    for k in range(1, owners):
        pl.semaphore_signal(barrier, inc=1, device_id={"own": (own + k) % owners}, device_id_type=MESH)
    pl.semaphore_wait(barrier, n + owners - 2)

    low = (z < depth_z // 2).astype(jnp.int32)

    def dest(s):
        if s == depth_z - 1:
            return z
        t = depth_z - 1 - s
        down_order = t - (z >= t).astype(jnp.int32)
        up_order = s + (z <= s).astype(jnp.int32)
        return low * down_order + (1 - low) * up_order

    steps = [(s, h) for s in range(depth_z) for h in range(halves)]

    def sub(h):
        return pl.ds(h * part, part)

    def send_x(i):
        s, h = steps[i]
        t = dest(s)
        return remote(grads.at[t, 1 - x, sub(h)], xbuf.at[t, sub(h)], xs.at[i], xr.at[i], "dp", partner)

    def send_up(t, h):
        return remote(mine.at[t, sub(h)], ubuf.at[t, sub(h)], us.at[t, h], ur.at[t, h], "dp", above)

    def send_down(t, h):
        return remote(mine.at[t, sub(h)], dbuf.at[t, sub(h)], ds.at[t, h], dr.at[t, h], "dp", below)

    def block(t, column, h):
        return g.at[pl.ds(pl.multiple_of((2 * t + column) * rows + h * part, part), part)]

    def gat_x(t, h):
        return remote(block(t, x, h), block(t, x, h), gxs.at[t, h], gxr.at[t, h], "dp", partner)

    def gat_up(t, h):
        return remote(block(t, x, h), block(t, x, h), gus.at[t, h], gur.at[t, h], "dp", above)

    def gat_down(t, h):
        return remote(block(t, x, h), block(t, x, h), gds.at[t, h], gdr.at[t, h], "dp", below)

    def root_x():
        return remote(rl_v.at[pl.ds(0, rows)], rl_v.at[pl.ds(rows, rows)], rxs.at[0], rxr.at[0], "dp", partner)

    def root_up(t):
        return remote(root_rows(t), root_rows(t), rus.at[t], rur.at[t], "dp", above)

    def root_down(t):
        return remote(root_rows(t), root_rows(t), rds.at[t], rdr.at[t], "dp", below)

    def root_event(k):
        if k == 0:
            @pl.when(has_above)
            def _():
                root_up(z).start()

            @pl.when(has_below)
            def _():
                root_down(z).start()
            return

        @pl.when(z >= k)
        def _():
            root_up(z - k).wait_recv()

            @pl.when(has_above)
            def _():
                root_up(z - k).start()

        @pl.when(z + k < depth_z)
        def _():
            root_down(z + k).wait_recv()

            @pl.when(has_below)
            def _():
                root_down(z + k).start()

    for i in range(min(DEPTH, len(steps))):
        send_x(i).start()
    load_rr.wait()
    root_event(0)
    load_mine.wait()

    for i, (s, h) in enumerate(steps):
        t = dest(s)
        send_x(i).wait_recv()
        if i + DEPTH < len(steps):
            send_x(i + DEPTH).start()
        if i == len(steps) - 1:
            loads[0].wait()
            root_x().start()
        rs = sub(h)
        acc = mine[t, rs].astype(F32) + xbuf[t, rs].astype(F32)
        if s < depth_z - 1:
            up, down = t > z, t < z

            @pl.when(up & has_below)
            def _():
                send_up(t, h).wait_recv()
                mine[t, rs] = (acc + ubuf[t, rs].astype(F32)).astype(BF16)

            @pl.when(down & has_above)
            def _():
                send_down(t, h).wait_recv()
                mine[t, rs] = (acc + dbuf[t, rs].astype(F32)).astype(BF16)

            @pl.when((up & (z == 0)) | (down & (z == depth_z - 1)))
            def _():
                mine[t, rs] = acc.astype(BF16)

            @pl.when(up)
            def _():
                send_up(t, h).start()

            @pl.when(down)
            def _():
                send_down(t, h).start()
        else:
            total[rs] = acc

            @pl.when(has_below)
            def _():
                send_up(t, h).wait_recv()
                total[rs] = total[rs] + ubuf[t, rs].astype(F32)

            @pl.when(has_above)
            def _():
                send_down(t, h).wait_recv()
                total[rs] = total[rs] + dbuf[t, rs].astype(F32)

            g[pl.ds(pl.multiple_of(me * rows + h * part, part), part)] = (total[rs] / n).astype(BF16)
            gat_x(z, h).start()

            @pl.when(has_above)
            def _():
                gat_up(z, h).start()

            @pl.when(has_below)
            def _():
                gat_down(z, h).start()
        if h == halves - 1 and s < (depth_z - 1) // 2:
            root_event(s + 1)

    for copy in loads[1:]:
        copy.wait()
    value = g[my_rows].astype(F32)
    one = 0.9 * first_v[...] + 0.1 * value
    two = 0.999 * second_v[...] + 0.001 * value * value
    first_v[...] = one
    second_v[...] = two
    adam = one / (jnp.sqrt(two) + 1e-08)
    adam_sq = jnp.sum(jnp.sum(adam * adam, axis=0, keepdims=True), axis=1, keepdims=True)
    stores = [
        pltpu.make_async_copy(src, dst.at[0], store_sem.at[i])
        for i, (src, dst) in enumerate(
            ((first_v, new_first), (second_v, new_second), (left_v, new_left), (right_v, new_right)))
    ]
    stores[0].start()
    stores[1].start()

    width = 256
    pair_rows = 2 * rows
    stepwise = pair_rows % LANES == 0

    def tile_of(i):
        return pl.ds(pl.multiple_of(i * width, width), width)

    def absorb(t, begin):
        for h in range(halves):
            gat_x(t, h).wait_recv()
        if not stepwise:
            return
        both = pl.ds(pl.multiple_of(t * pair_rows, pair_rows), pair_rows)

        def step(i, carry):
            c = tile_of(i)
            more = jnp.dot(rl_v[:, both], g[both, c], preferred_element_type=F32)
            inner[:, c] = more if begin else inner[:, c] + more
            return carry

        lax.fori_loop(0, size // width, step, 0)

    def absorb_at(k):
        if k == 0:
            root_x().wait_recv()
            absorb(z, True)
            return

        @pl.when(z >= k)
        def _():
            absorb(z - k, False)

        @pl.when(z + k < depth_z)
        def _():
            absorb(z + k, False)

    for k in range(1, depth_z):
        for h in range(halves):
            @pl.when(z >= k)
            def _():
                gat_up(z - k, h).wait_recv()
                gat_x(z - k, h).start()

                @pl.when(has_above)
                def _():
                    gat_up(z - k, h).start()

            @pl.when(z + k < depth_z)
            def _():
                gat_down(z + k, h).wait_recv()
                gat_x(z + k, h).start()

                @pl.when(has_below)
                def _():
                    gat_down(z + k, h).start()
        absorb_at(k - 1)
        late = (depth_z - 1) // 2 + k
        if late < depth_z - 1:
            root_event(late)
    absorb_at(depth_z - 1)
    if depth_z > 1:
        root_event(depth_z - 1)
    if not stepwise:
        def inner_step(i, carry):
            c = tile_of(i)
            inner[:, c] = jnp.dot(rl_v[...], g[:, c], preferred_element_type=F32)
            return carry

        lax.fori_loop(0, size // width, inner_step, 0)

    def parts_at(slot, cut):
        return parts.at[slot, x if cut == 0 else 1 - x]

    def swap():
        return remote(away, parts.at[own, x], axs.at[0], axr.at[0], "dp", partner)

    def to_pair(k, cut):
        here = parts_at(own, cut)
        return remote(here, here, ps.at[k, cut], pr.at[k, cut], "own", ((pair + k) % pairs) * 2 + core)

    def to_core(k, cut):
        here = parts_at(((pair + pairs - k) % pairs) * 2 + core, cut)
        return remote(here, here, cs.at[k, cut], cr.at[k, cut], "own", pair * 2 + 1 - core)

    precond_sq = jnp.zeros((1, 1), F32)
    rounded = inner[...].astype(BF16)
    for j in range(size // 2 // width):
        c = pl.ds(j * width, width)
        precond = lax.dot_general(
            rounded, right_rows[c, :], (((1,), (1,)), ((), ())), preferred_element_type=F32)
        parts[own, x, :, c] = precond[:rows].astype(BF16)
        away[:, c] = precond[rows:].astype(BF16)
        precond_sq += jnp.sum(
            jnp.sum(precond * precond, axis=0, keepdims=True), axis=1, keepdims=True)
    swap().start()
    for k in range(1, pairs):
        to_pair(k, 0).start()
    to_core(0, 0).start()

    line = lax.broadcasted_iota(jnp.int32, tile.shape, 0)
    tile[...] = jnp.where(line == 0, adam_sq, precond_sq)
    stats[me] = tile[...]

    def norm_to(k):
        return remote(tile, stats.at[me], ss.at[k], sr.at[k], "dp", (me + k) % n)

    for k in range(1, n):
        norm_to(k).start()

    def pass_half():
        swap().wait_recv()
        for k in range(1, pairs):
            to_pair(k, 1).start()
        to_core(0, 1).start()

    def left_step(i, carry):
        c = tile_of(i)
        outer = lax.dot_general(g[my_rows], g[c, :], (((1,), (1,)), ((), ())), preferred_element_type=F32)
        left_v[:, c] = 0.95 * left_v[:, c] + 0.05 * outer
        return carry

    lax.fori_loop(0, size // width, left_step, 0)
    stores[2].start()

    pass_half()
    for k in range(1, n):
        norm_to(k).wait_recv()
    sums = stats[0]
    for i in range(1, n):
        sums = sums + stats[i]
    scale = jnp.sqrt(sums[0:1]) / (jnp.sqrt(sums[1:2]) + 1e-06)
    scales[own] = jnp.broadcast_to(scale, scales.shape[1:])

    def scale_to(k):
        return remote(scales.at[own], scales.at[own], ts.at[k], tr.at[k], "own", (own + k) % owners)

    for k in range(1, owners):
        scale_to(k).start()

    for cut in range(cuts):
        for k in range(1, pairs):
            to_pair(k, cut).wait_recv()
            to_core(k, cut).start()

    aligned = pl.ds(pl.multiple_of(group * LANES, LANES), LANES)

    def turn_step(i, carry):
        r = pl.ds(pl.multiple_of(i * LANES, LANES), LANES)
        turned[:, r] = g[r, aligned].T
        return carry

    lax.fori_loop(0, groups, turn_step, 0)
    offset = pl.ds(pl.multiple_of(me * rows - group * LANES, 8), rows)

    def right_step(i, carry):
        c = tile_of(i)
        product[...] = jnp.dot(turned[...], g[:, c], preferred_element_type=F32)
        right_v[:, c] = 0.95 * right_v[:, c] + 0.05 * product[offset]
        return carry

    lax.fori_loop(0, size // width, right_step, 0)
    stores[3].start()

    for k in range(1, owners):
        scale_to(k).wait_recv()
    for cut in range(cuts):
        for k in range(pairs):
            to_core(k, cut).wait_recv()
    for b in range(owners):
        factor = scales[owner[b]][0:1, 0:1]
        for column in range(2):
            scaled = (parts[owner[b], column].astype(F32) * factor).astype(BF16)
            if rows % LANES:
                direction[b, :, pl.ds(column * (size // 2), size // 2)] = scaled
                continue
            for t in range(depth_z):
                direction[b, :, pl.ds((2 * t + column) * rows, rows)] = scaled[:, t * rows:(t + 1) * rows]

    for i, (s, h) in enumerate(steps):
        send_x(i).wait_send()
        gat_x(s, h).wait_send()
    for t in range(depth_z):
        for h in range(halves):
            @pl.when(z < t)
            def _():
                send_up(t, h).wait_send()

            @pl.when(z > t)
            def _():
                send_down(t, h).wait_send()

            @pl.when((z >= t) & has_above)
            def _():
                gat_up(t, h).wait_send()

            @pl.when((z <= t) & has_below)
            def _():
                gat_down(t, h).wait_send()
        @pl.when((z >= t) & has_above)
        def _():
            root_up(t).wait_send()

        @pl.when((z <= t) & has_below)
        def _():
            root_down(t).wait_send()
    root_x().wait_send()
    swap().wait_send()
    for k in range(1, n):
        norm_to(k).wait_send()
    for k in range(1, owners):
        scale_to(k).wait_send()
    for cut in range(cuts):
        for k in range(pairs):
            to_core(k, cut).wait_send()
            if k:
                to_pair(k, cut).wait_send()
    for copy in stores:
        copy.wait()


def finish_kernel(count, *refs):
    sources, targets, holds = refs[:count], refs[count:2 * count], refs[2 * count:3 * count]
    in_sem, out_sem = refs[3 * count:]
    copies = []
    for source, target, hold in zip(sources, targets, holds):
        blocks, rows, _ = source.shape
        cut = rows // 2 if blocks == 1 else rows
        for b in range(blocks):
            for at in range(0, rows, cut):
                piece = (b, pl.ds(at, cut))
                i = len(copies)
                copies.append((
                    pltpu.make_async_copy(source.at[piece], hold.at[piece], in_sem.at[i]),
                    pltpu.make_async_copy(hold.at[piece], target.at[piece], out_sem.at[i])))
    for load, _ in copies:
        load.start()
    for load, store in copies:
        load.wait()
        store.start()
    for _, store in copies:
        store.wait()


def finish(*arrays):
    count = len(arrays)
    pieces = sum(max(2, a.shape[0]) for a in arrays)
    anywhere = pl.BlockSpec(memory_space=pl.ANY)
    return pl.pallas_call(
        functools.partial(finish_kernel, count),
        out_shape=tuple(jax.ShapeDtypeStruct(a.shape, a.dtype) for a in arrays),
        in_specs=[anywhere] * count,
        out_specs=(anywhere,) * count,
        scratch_shapes=[pltpu.VMEM(a.shape, a.dtype) for a in arrays]
        + [pltpu.SemaphoreType.DMA((pieces,))] * 2,
        compiler_params=pltpu.CompilerParams(vmem_limit_bytes=VMEM),
    )(*arrays)


def body(n, owners, grads, left, right, root_left, root_right, first, second, owner):
    rows, size = left.shape[1:]
    line = n // 2
    halves = max(1, rows // 64)
    cuts = 2
    pairs = owners // 2
    sem = pltpu.SemaphoreType.DMA
    stat = jax.ShapeDtypeStruct((1, rows, size), F32)
    anywhere = pl.BlockSpec(memory_space=pl.ANY)
    hbm = pl.BlockSpec(memory_space=pltpu.HBM)
    *state, direction = pl.pallas_call(
        functools.partial(kernel, n, owners, halves, cuts),
        out_shape=(stat, stat, stat, stat, jax.ShapeDtypeStruct((owners, rows, size), BF16)),
        in_specs=[hbm] * 7 + [pl.BlockSpec(memory_space=pltpu.SMEM)],
        out_specs=(anywhere,) * 4 + (pl.BlockSpec(memory_space=pltpu.VMEM),),
        scratch_shapes=[
            *[pltpu.VMEM((line, rows, size), BF16)] * 4,
            pltpu.VMEM((rows, size), F32),
            pltpu.VMEM((size, size), BF16),
            pltpu.VMEM((size // 2, size), BF16),
            pltpu.VMEM((rows, size), F32),
            pltpu.VMEM((rows, size), F32),
            pltpu.VMEM((2 * rows, size), BF16),
            pltpu.VMEM((rows, size), F32),
            pltpu.VMEM((rows, size), F32),
            pltpu.VMEM((2 * rows, size), F32),
            pltpu.VMEM((LANES, size), BF16),
            pltpu.VMEM((LANES, 256), F32),
            pltpu.VMEM((owners, 2, rows, size // 2), BF16),
            pltpu.VMEM((rows, size // 2), BF16),
            pltpu.VMEM((8, LANES), F32),
            pltpu.VMEM((n, 8, LANES), F32),
            pltpu.VMEM((owners, 8, LANES), F32),
            sem((7,)), sem((4,)),
            sem((line * halves,)), sem((line * halves,)),
            *[sem((line, halves))] * 10,
            sem((1,)), sem((1,)),
            *[sem((line,))] * 4,
            sem((1,)), sem((1,)),
            *[sem((pairs, cuts))] * 4,
            sem((n,)), sem((n,)), sem((owners,)), sem((owners,)),
        ],
        compiler_params=pltpu.CompilerParams(
            collective_id=0, has_side_effects=True, vmem_limit_bytes=VMEM),
        cost_estimate=pl.CostEstimate(
            flops=8 * rows * size * size, bytes_accessed=24 * rows * size, transcendentals=rows * size),
    )(grads.reshape(line, 2, rows, size), left, right, root_left, root_right, first, second, owner)
    if rows % LANES:
        direction = direction.reshape(owners, rows, 2, line, rows).swapaxes(2, 3).reshape(owners, rows, size)
    return finish(*state, direction)


def solution(mesh):
    split = P("own", "dp", None)
    return jax.shard_map(
        functools.partial(body, mesh.shape["dp"], mesh.shape["own"]),
        mesh=mesh,
        in_specs=(P("dp", "own", None, None),) + (split,) * 6 + (P(),),
        out_specs=(split,) * 4 + (P(None, "dp", None),),
        check_vma=False,
    )
```

```python
import functools

import jax
import jax.numpy as jnp
from jax import lax
from jax.experimental import pallas as pl
from jax.experimental.pallas import tpu as pltpu
from jax.sharding import PartitionSpec as P

MESH = pl.DeviceIdType.MESH
F32 = jnp.float32
BF16 = jnp.bfloat16
LANES = 128
DEPTH = 3
VMEM = 60 * 1024 * 1024


def remote(src, dst, send, recv, axis, to):
    return pltpu.make_async_remote_copy(
        src_ref=src, dst_ref=dst, send_sem=send, recv_sem=recv,
        device_id={axis: to}, device_id_type=MESH,
    )


def kernel(n, owners, halves, cuts, grads, left, right, root_left, root_right, first, second, owner,
           new_left, new_right, new_first, new_second, direction,
           mine, xbuf, ubuf, dbuf, tmine, tub, tdb, tx, total, g, right_rows, left_v, right_v, rl_v, first_v, second_v,
           inner, turned, product, parts, away, tile, stats, scales,
           load_sem, store_sem, xs, xr, us, ur, ds, dr, gxs, gxr, gus, gur, gds, gdr,
           rxs, rxr, rus, rur, rds, rdr, axs, axr, ps, pr, cs, cr, ss, sr, ts, tr,
           tus, tur, tds, tdr, txs, txr, hxs, hxr, hus, hur, hds, hdr):
    me = lax.axis_index("dp")
    own = lax.axis_index("own")
    size = g.shape[0]
    rows = left_v.shape[0]
    depth_z = n // 2
    z, x = me // 2, me % 2
    partner, above, below = z * 2 + 1 - x, me + 2, me - 2
    pairs = owners // 2
    pair, core = own // 2, own % 2
    part = rows // halves
    groups = size // LANES
    has_above, has_below = z < depth_z - 1, z > 0

    head, tail = pl.ds(0, size - LANES), pl.ds(size - LANES, LANES)

    def root_rows(t):
        return right_rows.at[pl.ds(pl.multiple_of(t * rows, rows), rows)]

    load_mine = pltpu.make_async_copy(grads.at[:, x], mine, load_sem.at[0])
    loads = [
        pltpu.make_async_copy(src.at[0], dst, load_sem.at[i + 1])
        for i, (src, dst) in enumerate(
            ((root_left, rl_v.at[pl.ds(0, rows)]), (first, first_v), (second, second_v), (left, left_v), (right, right_v)))
    ]
    my_rows = pl.ds(pl.multiple_of(me * rows, rows), rows)
    group = (me * rows) // LANES
    load_rr = pltpu.make_async_copy(root_right.at[0], root_rows(z), load_sem.at[6])
    load_rr.start()
    load_tail = pltpu.make_async_copy(grads.at[:, 1 - x, :, tail], tmine, load_sem.at[7])
    load_mine.start()
    load_tail.start()
    for copy in loads:
        copy.start()

    barrier = pltpu.get_barrier_semaphore()
    for k in range(1, n):
        pl.semaphore_signal(barrier, inc=1, device_id={"dp": (me + k) % n}, device_id_type=MESH)
    for k in range(1, owners):
        pl.semaphore_signal(barrier, inc=1, device_id={"own": (own + k) % owners}, device_id_type=MESH)
    pl.semaphore_wait(barrier, n + owners - 2)

    low = (z < depth_z // 2).astype(jnp.int32)

    def dest(s):
        if s == depth_z - 1:
            return z
        t = depth_z - 1 - s
        down_order = t - (z >= t).astype(jnp.int32)
        up_order = s + (z <= s).astype(jnp.int32)
        return low * down_order + (1 - low) * up_order

    steps = [(s, h) for s in range(depth_z) for h in range(halves)]

    def sub(h):
        return pl.ds(h * part, part)

    def send_x(i):
        s, h = steps[i]
        t = dest(s)
        return remote(grads.at[t, 1 - x, sub(h), head], xbuf.at[t, sub(h), head], xs.at[i], xr.at[i], "dp", partner)

    def send_up(t, h):
        return remote(mine.at[t, sub(h)], ubuf.at[t, sub(h)], us.at[t, h], ur.at[t, h], "dp", above)

    def send_down(t, h):
        return remote(mine.at[t, sub(h)], dbuf.at[t, sub(h)], ds.at[t, h], dr.at[t, h], "dp", below)

    def tail_up(t):
        return remote(tmine.at[t], tub.at[t], tus.at[t], tur.at[t], "dp", above)

    def tail_down(t):
        return remote(tmine.at[t], tdb.at[t], tds.at[t], tdr.at[t], "dp", below)

    def tail_x():
        return remote(tmine.at[z], tx, txs.at[0], txr.at[0], "dp", partner)

    def tail_step(s):
        t = dest(s)
        if s < depth_z - 1:
            @pl.when((t > z) & has_below)
            def _():
                tail_up(t).wait_recv()
                tmine[t] = (tmine[t].astype(F32) + tub[t].astype(F32)).astype(BF16)

            @pl.when((t < z) & has_above)
            def _():
                tail_down(t).wait_recv()
                tmine[t] = (tmine[t].astype(F32) + tdb[t].astype(F32)).astype(BF16)

            @pl.when(t > z)
            def _():
                tail_up(t).start()

            @pl.when(t < z)
            def _():
                tail_down(t).start()
            return

        @pl.when(has_below)
        def _():
            tail_up(z).wait_recv()
            tmine[z] = (tmine[z].astype(F32) + tub[z].astype(F32)).astype(BF16)

        @pl.when(has_above)
        def _():
            tail_down(z).wait_recv()
            tmine[z] = (tmine[z].astype(F32) + tdb[z].astype(F32)).astype(BF16)

        tail_x().start()

    def block(t, column, h):
        return g.at[pl.ds(pl.multiple_of((2 * t + column) * rows + h * part, part), part)]

    def gat_x(t, h):
        here = block(t, x, h).at[:, head]
        return remote(here, here, gxs.at[t, h], gxr.at[t, h], "dp", partner)

    def end_x(h):
        here = block(z, x, h).at[:, tail]
        return remote(here, here, hxs.at[h], hxr.at[h], "dp", partner)

    def end_up(t, h):
        here = block(t, 1 - x, h).at[:, tail]
        return remote(here, here, hus.at[t, h], hur.at[t, h], "dp", above)

    def end_down(t, h):
        here = block(t, 1 - x, h).at[:, tail]
        return remote(here, here, hds.at[t, h], hdr.at[t, h], "dp", below)

    def end_event(k):
        for h in range(halves):
            if k == 0:
                end_x(h).wait_recv()

                @pl.when(has_above)
                def _():
                    end_up(z, h).start()

                @pl.when(has_below)
                def _():
                    end_down(z, h).start()
                continue

            @pl.when(z >= k)
            def _():
                end_up(z - k, h).wait_recv()

                @pl.when(has_above)
                def _():
                    end_up(z - k, h).start()

            @pl.when(z + k < depth_z)
            def _():
                end_down(z + k, h).wait_recv()

                @pl.when(has_below)
                def _():
                    end_down(z + k, h).start()

    def gat_up(t, h):
        return remote(block(t, x, h), block(t, x, h), gus.at[t, h], gur.at[t, h], "dp", above)

    def gat_down(t, h):
        return remote(block(t, x, h), block(t, x, h), gds.at[t, h], gdr.at[t, h], "dp", below)

    def root_x():
        return remote(rl_v.at[pl.ds(0, rows)], rl_v.at[pl.ds(rows, rows)], rxs.at[0], rxr.at[0], "dp", partner)

    def root_up(t):
        return remote(root_rows(t), root_rows(t), rus.at[t], rur.at[t], "dp", above)

    def root_down(t):
        return remote(root_rows(t), root_rows(t), rds.at[t], rdr.at[t], "dp", below)

    def root_event(k):
        if k == 0:
            @pl.when(has_above)
            def _():
                root_up(z).start()

            @pl.when(has_below)
            def _():
                root_down(z).start()
            return

        @pl.when(z >= k)
        def _():
            root_up(z - k).wait_recv()

            @pl.when(has_above)
            def _():
                root_up(z - k).start()

        @pl.when(z + k < depth_z)
        def _():
            root_down(z + k).wait_recv()

            @pl.when(has_below)
            def _():
                root_down(z + k).start()

    for i in range(min(DEPTH, len(steps))):
        send_x(i).start()
    load_rr.wait()
    root_event(0)
    xbuf[:, :, tail] = jnp.zeros((depth_z, rows, LANES), BF16)
    load_mine.wait()
    load_tail.wait()

    for i, (s, h) in enumerate(steps):
        t = dest(s)
        if h == 0:
            tail_step(s)
        send_x(i).wait_recv()
        if i + DEPTH < len(steps):
            send_x(i + DEPTH).start()
        if i == len(steps) - 1:
            loads[0].wait()
            root_x().start()
        rs = sub(h)
        acc = mine[t, rs].astype(F32) + xbuf[t, rs].astype(F32)
        if s < depth_z - 1:
            up, down = t > z, t < z

            @pl.when(up & has_below)
            def _():
                send_up(t, h).wait_recv()
                mine[t, rs] = (acc + ubuf[t, rs].astype(F32)).astype(BF16)

            @pl.when(down & has_above)
            def _():
                send_down(t, h).wait_recv()
                mine[t, rs] = (acc + dbuf[t, rs].astype(F32)).astype(BF16)

            @pl.when((up & (z == 0)) | (down & (z == depth_z - 1)))
            def _():
                mine[t, rs] = acc.astype(BF16)

            @pl.when(up)
            def _():
                send_up(t, h).start()

            @pl.when(down)
            def _():
                send_down(t, h).start()
        else:
            total[rs] = acc

            @pl.when(has_below)
            def _():
                send_up(t, h).wait_recv()
                total[rs] = total[rs] + ubuf[t, rs].astype(F32)

            @pl.when(has_above)
            def _():
                send_down(t, h).wait_recv()
                total[rs] = total[rs] + dbuf[t, rs].astype(F32)

            if h == 0:
                tail_x().wait_recv()
            total[rs, tail] = total[rs, tail] + tx[rs].astype(F32)
            g[pl.ds(pl.multiple_of(me * rows + h * part, part), part)] = (total[rs] / n).astype(BF16)
            end_x(h).start()
            gat_x(z, h).start()

            @pl.when(has_above)
            def _():
                gat_up(z, h).start()

            @pl.when(has_below)
            def _():
                gat_down(z, h).start()
        if h == halves - 1 and s < (depth_z - 1) // 2:
            root_event(s + 1)

    for copy in loads[1:]:
        copy.wait()
    value = g[my_rows].astype(F32)
    one = 0.9 * first_v[...] + 0.1 * value
    two = 0.999 * second_v[...] + 0.001 * value * value
    first_v[...] = one
    second_v[...] = two
    adam = one / (jnp.sqrt(two) + 1e-08)
    adam_sq = jnp.sum(jnp.sum(adam * adam, axis=0, keepdims=True), axis=1, keepdims=True)
    stores = [
        pltpu.make_async_copy(src, dst.at[0], store_sem.at[i])
        for i, (src, dst) in enumerate(
            ((first_v, new_first), (second_v, new_second), (left_v, new_left), (right_v, new_right)))
    ]
    stores[0].start()
    stores[1].start()

    width = 256
    pair_rows = 2 * rows
    stepwise = pair_rows % LANES == 0

    def tile_of(i):
        return pl.ds(pl.multiple_of(i * width, width), width)

    def absorb(t, begin):
        for h in range(halves):
            gat_x(t, h).wait_recv()
        if not stepwise:
            return
        both = pl.ds(pl.multiple_of(t * pair_rows, pair_rows), pair_rows)

        def step(i, carry):
            c = tile_of(i)
            more = jnp.dot(rl_v[:, both], g[both, c], preferred_element_type=F32)
            inner[:, c] = more if begin else inner[:, c] + more
            return carry

        lax.fori_loop(0, size // width, step, 0)

    def absorb_at(k):
        if k == 0:
            root_x().wait_recv()
            absorb(z, True)
            return

        @pl.when(z >= k)
        def _():
            absorb(z - k, False)

        @pl.when(z + k < depth_z)
        def _():
            absorb(z + k, False)

    end_event(0)
    for k in range(1, depth_z):
        for h in range(halves):
            @pl.when(z >= k)
            def _():
                gat_up(z - k, h).wait_recv()
                gat_x(z - k, h).start()

                @pl.when(has_above)
                def _():
                    gat_up(z - k, h).start()

            @pl.when(z + k < depth_z)
            def _():
                gat_down(z + k, h).wait_recv()
                gat_x(z + k, h).start()

                @pl.when(has_below)
                def _():
                    gat_down(z + k, h).start()
        end_event(k)
        absorb_at(k - 1)
        late = (depth_z - 1) // 2 + k
        if late < depth_z - 1:
            root_event(late)
    absorb_at(depth_z - 1)
    if depth_z > 1:
        root_event(depth_z - 1)
    if not stepwise:
        def inner_step(i, carry):
            c = tile_of(i)
            inner[:, c] = jnp.dot(rl_v[...], g[:, c], preferred_element_type=F32)
            return carry

        lax.fori_loop(0, size // width, inner_step, 0)

    def parts_at(slot, cut):
        return parts.at[slot, x if cut == 0 else 1 - x]

    def swap():
        return remote(away, parts.at[own, x], axs.at[0], axr.at[0], "dp", partner)

    def to_pair(k, cut):
        here = parts_at(own, cut)
        return remote(here, here, ps.at[k, cut], pr.at[k, cut], "own", ((pair + k) % pairs) * 2 + core)

    def to_core(k, cut):
        here = parts_at(((pair + pairs - k) % pairs) * 2 + core, cut)
        return remote(here, here, cs.at[k, cut], cr.at[k, cut], "own", pair * 2 + 1 - core)

    precond_sq = jnp.zeros((1, 1), F32)
    rounded = inner[...].astype(BF16)
    for j in range(size // 2 // width):
        c = pl.ds(j * width, width)
        precond = lax.dot_general(
            rounded, right_rows[c, :], (((1,), (1,)), ((), ())), preferred_element_type=F32)
        parts[own, x, :, c] = precond[:rows].astype(BF16)
        away[:, c] = precond[rows:].astype(BF16)
        precond_sq += jnp.sum(
            jnp.sum(precond * precond, axis=0, keepdims=True), axis=1, keepdims=True)
    swap().start()
    for k in range(1, pairs):
        to_pair(k, 0).start()
    to_core(0, 0).start()

    line = lax.broadcasted_iota(jnp.int32, tile.shape, 0)
    tile[...] = jnp.where(line == 0, adam_sq, precond_sq)
    stats[me] = tile[...]

    def norm_to(k):
        return remote(tile, stats.at[me], ss.at[k], sr.at[k], "dp", (me + k) % n)

    for k in range(1, n):
        norm_to(k).start()

    def pass_half():
        swap().wait_recv()
        for k in range(1, pairs):
            to_pair(k, 1).start()
        to_core(0, 1).start()

    def left_step(i, carry):
        c = tile_of(i)
        outer = lax.dot_general(g[my_rows], g[c, :], (((1,), (1,)), ((), ())), preferred_element_type=F32)
        left_v[:, c] = 0.95 * left_v[:, c] + 0.05 * outer
        return carry

    lax.fori_loop(0, size // width, left_step, 0)
    stores[2].start()

    pass_half()
    for k in range(1, n):
        norm_to(k).wait_recv()
    sums = stats[0]
    for i in range(1, n):
        sums = sums + stats[i]
    scale = jnp.sqrt(sums[0:1]) / (jnp.sqrt(sums[1:2]) + 1e-06)
    scales[own] = jnp.broadcast_to(scale, scales.shape[1:])

    def scale_to(k):
        return remote(scales.at[own], scales.at[own], ts.at[k], tr.at[k], "own", (own + k) % owners)

    for k in range(1, owners):
        scale_to(k).start()

    for cut in range(cuts):
        for k in range(1, pairs):
            to_pair(k, cut).wait_recv()
            to_core(k, cut).start()

    aligned = pl.ds(pl.multiple_of(group * LANES, LANES), LANES)

    def turn_step(i, carry):
        r = pl.ds(pl.multiple_of(i * LANES, LANES), LANES)
        turned[:, r] = g[r, aligned].T
        return carry

    lax.fori_loop(0, groups, turn_step, 0)
    offset = pl.ds(pl.multiple_of(me * rows - group * LANES, 8), rows)

    def right_step(i, carry):
        c = tile_of(i)
        product[...] = jnp.dot(turned[...], g[:, c], preferred_element_type=F32)
        right_v[:, c] = 0.95 * right_v[:, c] + 0.05 * product[offset]
        return carry

    lax.fori_loop(0, size // width, right_step, 0)
    stores[3].start()

    for k in range(1, owners):
        scale_to(k).wait_recv()
    for cut in range(cuts):
        for k in range(pairs):
            to_core(k, cut).wait_recv()
    for b in range(owners):
        factor = scales[owner[b]][0:1, 0:1]
        for column in range(2):
            scaled = (parts[owner[b], column].astype(F32) * factor).astype(BF16)
            if rows % LANES:
                direction[b, :, pl.ds(column * (size // 2), size // 2)] = scaled
                continue
            for t in range(depth_z):
                direction[b, :, pl.ds((2 * t + column) * rows, rows)] = scaled[:, t * rows:(t + 1) * rows]

    for i, (s, h) in enumerate(steps):
        send_x(i).wait_send()
        gat_x(s, h).wait_send()
    for t in range(depth_z):
        for h in range(halves):
            @pl.when((z >= t) & has_above)
            def _():
                end_up(t, h).wait_send()

            @pl.when((z <= t) & has_below)
            def _():
                end_down(t, h).wait_send()

            @pl.when(z < t)
            def _():
                send_up(t, h).wait_send()

            @pl.when(z > t)
            def _():
                send_down(t, h).wait_send()

            @pl.when((z >= t) & has_above)
            def _():
                gat_up(t, h).wait_send()

            @pl.when((z <= t) & has_below)
            def _():
                gat_down(t, h).wait_send()
        @pl.when(z < t)
        def _():
            tail_up(t).wait_send()

        @pl.when(z > t)
        def _():
            tail_down(t).wait_send()

        @pl.when((z >= t) & has_above)
        def _():
            root_up(t).wait_send()

        @pl.when((z <= t) & has_below)
        def _():
            root_down(t).wait_send()
    root_x().wait_send()
    tail_x().wait_send()
    for h in range(halves):
        end_x(h).wait_send()
    swap().wait_send()
    for k in range(1, n):
        norm_to(k).wait_send()
    for k in range(1, owners):
        scale_to(k).wait_send()
    for cut in range(cuts):
        for k in range(pairs):
            to_core(k, cut).wait_send()
            if k:
                to_pair(k, cut).wait_send()
    for copy in stores:
        copy.wait()


def finish_kernel(count, *refs):
    sources, targets, holds = refs[:count], refs[count:2 * count], refs[2 * count:3 * count]
    in_sem, out_sem = refs[3 * count:]
    copies = []
    for source, target, hold in zip(sources, targets, holds):
        blocks, rows, _ = source.shape
        cut = rows // 2 if blocks == 1 else rows
        for b in range(blocks):
            for at in range(0, rows, cut):
                piece = (b, pl.ds(at, cut))
                i = len(copies)
                copies.append((
                    pltpu.make_async_copy(source.at[piece], hold.at[piece], in_sem.at[i]),
                    pltpu.make_async_copy(hold.at[piece], target.at[piece], out_sem.at[i])))
    for load, _ in copies:
        load.start()
    for load, store in copies:
        load.wait()
        store.start()
    for _, store in copies:
        store.wait()


def finish(*arrays):
    count = len(arrays)
    pieces = sum(max(2, a.shape[0]) for a in arrays)
    anywhere = pl.BlockSpec(memory_space=pl.ANY)
    return pl.pallas_call(
        functools.partial(finish_kernel, count),
        out_shape=tuple(jax.ShapeDtypeStruct(a.shape, a.dtype) for a in arrays),
        in_specs=[anywhere] * count,
        out_specs=(anywhere,) * count,
        scratch_shapes=[pltpu.VMEM(a.shape, a.dtype) for a in arrays]
        + [pltpu.SemaphoreType.DMA((pieces,))] * 2,
        compiler_params=pltpu.CompilerParams(vmem_limit_bytes=VMEM),
    )(*arrays)


def body(n, owners, grads, left, right, root_left, root_right, first, second, owner):
    rows, size = left.shape[1:]
    line = n // 2
    halves = max(1, rows // 64)
    cuts = 2
    pairs = owners // 2
    sem = pltpu.SemaphoreType.DMA
    stat = jax.ShapeDtypeStruct((1, rows, size), F32)
    anywhere = pl.BlockSpec(memory_space=pl.ANY)
    hbm = pl.BlockSpec(memory_space=pltpu.HBM)
    *state, direction = pl.pallas_call(
        functools.partial(kernel, n, owners, halves, cuts),
        out_shape=(stat, stat, stat, stat, jax.ShapeDtypeStruct((owners, rows, size), BF16)),
        in_specs=[hbm] * 7 + [pl.BlockSpec(memory_space=pltpu.SMEM)],
        out_specs=(anywhere,) * 4 + (pl.BlockSpec(memory_space=pltpu.VMEM),),
        scratch_shapes=[
            *[pltpu.VMEM((line, rows, size), BF16)] * 4,
            *[pltpu.VMEM((line, rows, LANES), BF16)] * 3,
            pltpu.VMEM((rows, LANES), BF16),
            pltpu.VMEM((rows, size), F32),
            pltpu.VMEM((size, size), BF16),
            pltpu.VMEM((size // 2, size), BF16),
            pltpu.VMEM((rows, size), F32),
            pltpu.VMEM((rows, size), F32),
            pltpu.VMEM((2 * rows, size), BF16),
            pltpu.VMEM((rows, size), F32),
            pltpu.VMEM((rows, size), F32),
            pltpu.VMEM((2 * rows, size), F32),
            pltpu.VMEM((LANES, size), BF16),
            pltpu.VMEM((LANES, 256), F32),
            pltpu.VMEM((owners, 2, rows, size // 2), BF16),
            pltpu.VMEM((rows, size // 2), BF16),
            pltpu.VMEM((8, LANES), F32),
            pltpu.VMEM((n, 8, LANES), F32),
            pltpu.VMEM((owners, 8, LANES), F32),
            sem((8,)), sem((4,)),
            sem((line * halves,)), sem((line * halves,)),
            *[sem((line, halves))] * 10,
            sem((1,)), sem((1,)),
            *[sem((line,))] * 4,
            sem((1,)), sem((1,)),
            *[sem((pairs, cuts))] * 4,
            sem((n,)), sem((n,)), sem((owners,)), sem((owners,)),
            *[sem((line,))] * 4,
            sem((1,)), sem((1,)), sem((halves,)), sem((halves,)),
            *[sem((line, halves))] * 4,
        ],
        compiler_params=pltpu.CompilerParams(
            collective_id=0, has_side_effects=True, vmem_limit_bytes=VMEM),
        cost_estimate=pl.CostEstimate(
            flops=8 * rows * size * size, bytes_accessed=24 * rows * size, transcendentals=rows * size),
    )(grads.reshape(line, 2, rows, size), left, right, root_left, root_right, first, second, owner)
    if rows % LANES:
        direction = direction.reshape(owners, rows, 2, line, rows).swapaxes(2, 3).reshape(owners, rows, size)
    return finish(*state, direction)


def solution(mesh):
    split = P("own", "dp", None)
    return jax.shard_map(
        functools.partial(body, mesh.shape["dp"], mesh.shape["own"]),
        mesh=mesh,
        in_specs=(P("dp", "own", None, None),) + (split,) * 6 + (P(),),
        out_specs=(split,) * 4 + (P(None, "dp", None),),
        check_vma=False,
    )
```

```python
import functools

import jax
import jax.numpy as jnp
from jax import lax
from jax.experimental import pallas as pl
from jax.experimental.pallas import tpu as pltpu
from jax.sharding import PartitionSpec as P

MESH = pl.DeviceIdType.MESH
F32 = jnp.float32
BF16 = jnp.bfloat16
LANES = 128
DEPTH = 3
VMEM = 60 * 1024 * 1024


def remote(src, dst, send, recv, axis, to):
    return pltpu.make_async_remote_copy(
        src_ref=src, dst_ref=dst, send_sem=send, recv_sem=recv,
        device_id={axis: to}, device_id_type=MESH,
    )


def kernel(n, owners, halves, cuts, grads, left, right, root_left, root_right, first, second, owner,
           new_left, new_right, new_first, new_second, direction,
           mine, xbuf, ubuf, dbuf, total, g, right_rows, left_v, right_v, rl_v, first_v, second_v,
           inner, turned, product, parts, scaled_v, away, tile, stats, scales,
           load_sem, store_sem, xs, xr, us, ur, ds, dr, gxs, gxr, gus, gur, gds, gdr,
           rxs, rxr, rus, rur, rds, rdr, axs, axr, ps, pr, cs, cr, ss, sr, ts, tr):
    me = lax.axis_index("dp")
    own = lax.axis_index("own")
    size = g.shape[0]
    rows = left_v.shape[0]
    depth_z = n // 2
    z, x = me // 2, me % 2
    partner, above, below = z * 2 + 1 - x, me + 2, me - 2
    pairs = owners // 2
    pair, core = own // 2, own % 2
    part = rows // halves
    groups = size // LANES
    has_above, has_below = z < depth_z - 1, z > 0

    def root_rows(t):
        return right_rows.at[pl.ds(pl.multiple_of(t * rows, rows), rows)]

    load_mine = pltpu.make_async_copy(grads.at[:, x], mine, load_sem.at[0])
    loads = [
        pltpu.make_async_copy(src.at[0], dst, load_sem.at[i + 1])
        for i, (src, dst) in enumerate(
            ((root_left, rl_v.at[pl.ds(0, rows)]), (first, first_v), (second, second_v), (left, left_v), (right, right_v)))
    ]
    my_rows = pl.ds(pl.multiple_of(me * rows, rows), rows)
    group = (me * rows) // LANES
    load_rr = pltpu.make_async_copy(root_right.at[0], root_rows(z), load_sem.at[6])
    load_rr.start()
    load_mine.start()
    for copy in loads:
        copy.start()

    barrier = pltpu.get_barrier_semaphore()
    for k in range(1, n):
        pl.semaphore_signal(barrier, inc=1, device_id={"dp": (me + k) % n}, device_id_type=MESH)
    for k in range(1, owners):
        pl.semaphore_signal(barrier, inc=1, device_id={"own": (own + k) % owners}, device_id_type=MESH)
    pl.semaphore_wait(barrier, n + owners - 2)

    low = (z < depth_z // 2).astype(jnp.int32)

    def dest(s):
        if s == depth_z - 1:
            return z
        t = depth_z - 1 - s
        down_order = t - (z >= t).astype(jnp.int32)
        up_order = s + (z <= s).astype(jnp.int32)
        return low * down_order + (1 - low) * up_order

    steps = [(s, h) for s in range(depth_z) for h in range(halves)]

    def sub(h):
        return pl.ds(h * part, part)

    def send_x(i):
        s, h = steps[i]
        t = dest(s)
        return remote(grads.at[t, 1 - x, sub(h)], xbuf.at[t, sub(h)], xs.at[i], xr.at[i], "dp", partner)

    def send_up(t, h):
        return remote(mine.at[t, sub(h)], ubuf.at[t, sub(h)], us.at[t, h], ur.at[t, h], "dp", above)

    def send_down(t, h):
        return remote(mine.at[t, sub(h)], dbuf.at[t, sub(h)], ds.at[t, h], dr.at[t, h], "dp", below)

    def block(t, column, h):
        return g.at[pl.ds(pl.multiple_of((2 * t + column) * rows + h * part, part), part)]

    def gat_x(t, h):
        return remote(block(t, x, h), block(t, x, h), gxs.at[t, h], gxr.at[t, h], "dp", partner)

    def gat_up(t, h):
        return remote(block(t, x, h), block(t, x, h), gus.at[t, h], gur.at[t, h], "dp", above)

    def gat_down(t, h):
        return remote(block(t, x, h), block(t, x, h), gds.at[t, h], gdr.at[t, h], "dp", below)

    def root_x():
        return remote(rl_v.at[pl.ds(0, rows)], rl_v.at[pl.ds(rows, rows)], rxs.at[0], rxr.at[0], "dp", partner)

    def root_up(t):
        return remote(root_rows(t), root_rows(t), rus.at[t], rur.at[t], "dp", above)

    def root_down(t):
        return remote(root_rows(t), root_rows(t), rds.at[t], rdr.at[t], "dp", below)

    def root_event(k):
        if k == 0:
            @pl.when(has_above)
            def _():
                root_up(z).start()

            @pl.when(has_below)
            def _():
                root_down(z).start()
            return

        @pl.when(z >= k)
        def _():
            root_up(z - k).wait_recv()

            @pl.when(has_above)
            def _():
                root_up(z - k).start()

        @pl.when(z + k < depth_z)
        def _():
            root_down(z + k).wait_recv()

            @pl.when(has_below)
            def _():
                root_down(z + k).start()

    for i in range(min(DEPTH, len(steps))):
        send_x(i).start()
    load_rr.wait()
    root_event(0)
    load_mine.wait()

    for i, (s, h) in enumerate(steps):
        t = dest(s)
        send_x(i).wait_recv()
        if i + DEPTH < len(steps):
            send_x(i + DEPTH).start()
        if i == len(steps) - 1:
            loads[0].wait()
            root_x().start()
        rs = sub(h)
        acc = mine[t, rs].astype(F32) + xbuf[t, rs].astype(F32)
        if s < depth_z - 1:
            up, down = t > z, t < z

            @pl.when(up & has_below)
            def _():
                send_up(t, h).wait_recv()
                mine[t, rs] = (acc + ubuf[t, rs].astype(F32)).astype(BF16)

            @pl.when(down & has_above)
            def _():
                send_down(t, h).wait_recv()
                mine[t, rs] = (acc + dbuf[t, rs].astype(F32)).astype(BF16)

            @pl.when((up & (z == 0)) | (down & (z == depth_z - 1)))
            def _():
                mine[t, rs] = acc.astype(BF16)

            @pl.when(up)
            def _():
                send_up(t, h).start()

            @pl.when(down)
            def _():
                send_down(t, h).start()
        else:
            total[rs] = acc

            @pl.when(has_below)
            def _():
                send_up(t, h).wait_recv()
                total[rs] = total[rs] + ubuf[t, rs].astype(F32)

            @pl.when(has_above)
            def _():
                send_down(t, h).wait_recv()
                total[rs] = total[rs] + dbuf[t, rs].astype(F32)

            g[pl.ds(pl.multiple_of(me * rows + h * part, part), part)] = (total[rs] / n).astype(BF16)
            gat_x(z, h).start()

            @pl.when(has_above)
            def _():
                gat_up(z, h).start()

            @pl.when(has_below)
            def _():
                gat_down(z, h).start()
        if h == halves - 1 and s < (depth_z - 1) // 2:
            root_event(s + 1)

    for copy in loads[1:]:
        copy.wait()
    value = g[my_rows].astype(F32)
    one = 0.9 * first_v[...] + 0.1 * value
    two = 0.999 * second_v[...] + 0.001 * value * value
    first_v[...] = one
    second_v[...] = two
    adam = one / (jnp.sqrt(two) + 1e-08)
    adam_sq = jnp.sum(jnp.sum(adam * adam, axis=0, keepdims=True), axis=1, keepdims=True)
    stores = [
        pltpu.make_async_copy(src, dst.at[0], store_sem.at[i])
        for i, (src, dst) in enumerate(
            ((first_v, new_first), (second_v, new_second), (left_v, new_left), (right_v, new_right)))
    ]
    stores[0].start()
    stores[1].start()

    width = 256
    pair_rows = 2 * rows
    stepwise = pair_rows % LANES == 0

    def tile_of(i):
        return pl.ds(pl.multiple_of(i * width, width), width)

    def absorb(t, begin):
        for h in range(halves):
            gat_x(t, h).wait_recv()
        if not stepwise:
            return
        both = pl.ds(pl.multiple_of(t * pair_rows, pair_rows), pair_rows)

        def step(i, carry):
            c = tile_of(i)
            more = jnp.dot(rl_v[:, both], g[both, c], preferred_element_type=F32)
            inner[:, c] = more if begin else inner[:, c] + more
            return carry

        lax.fori_loop(0, size // width, step, 0)

    def absorb_at(k):
        if k == 0:
            root_x().wait_recv()
            absorb(z, True)
            return

        @pl.when(z >= k)
        def _():
            absorb(z - k, False)

        @pl.when(z + k < depth_z)
        def _():
            absorb(z + k, False)

    for k in range(1, depth_z):
        for h in range(halves):
            @pl.when(z >= k)
            def _():
                gat_up(z - k, h).wait_recv()
                gat_x(z - k, h).start()

                @pl.when(has_above)
                def _():
                    gat_up(z - k, h).start()

            @pl.when(z + k < depth_z)
            def _():
                gat_down(z + k, h).wait_recv()
                gat_x(z + k, h).start()

                @pl.when(has_below)
                def _():
                    gat_down(z + k, h).start()
        absorb_at(k - 1)
        late = (depth_z - 1) // 2 + k
        if late < depth_z - 1:
            root_event(late)
    absorb_at(depth_z - 1)
    if depth_z > 1:
        root_event(depth_z - 1)
    if not stepwise:
        def inner_step(i, carry):
            c = tile_of(i)
            inner[:, c] = jnp.dot(rl_v[...], g[:, c], preferred_element_type=F32)
            return carry

        lax.fori_loop(0, size // width, inner_step, 0)

    def parts_at(slot, cut):
        return parts.at[slot, x if cut == 0 else 1 - x]

    def swap():
        return remote(away, parts.at[own, x], axs.at[0], axr.at[0], "dp", partner)

    def to_pair(k, cut):
        here = parts_at(own, cut)
        return remote(here, here, ps.at[k, cut], pr.at[k, cut], "own", ((pair + k) % pairs) * 2 + core)

    def to_core(k, cut):
        here = parts_at(((pair + pairs - k) % pairs) * 2 + core, cut)
        return remote(here, here, cs.at[k, cut], cr.at[k, cut], "own", pair * 2 + 1 - core)

    precond_sq = jnp.zeros((1, 1), F32)
    rounded = inner[...].astype(BF16)
    for j in range(size // 2 // width):
        c = pl.ds(j * width, width)
        precond = lax.dot_general(
            rounded, right_rows[c, :], (((1,), (1,)), ((), ())), preferred_element_type=F32)
        parts[own, x, :, c] = precond[:rows].astype(BF16)
        away[:, c] = precond[rows:].astype(BF16)
        precond_sq += jnp.sum(
            jnp.sum(precond * precond, axis=0, keepdims=True), axis=1, keepdims=True)
    swap().start()
    for k in range(1, pairs):
        to_pair(k, 0).start()
    to_core(0, 0).start()

    line = lax.broadcasted_iota(jnp.int32, tile.shape, 0)
    tile[...] = jnp.where(line == 0, adam_sq, precond_sq)
    stats[me] = tile[...]

    def norm_to(k):
        return remote(tile, stats.at[me], ss.at[k], sr.at[k], "dp", (me + k) % n)

    for k in range(1, n):
        norm_to(k).start()

    def pass_half():
        swap().wait_recv()
        for k in range(1, pairs):
            to_pair(k, 1).start()
        to_core(0, 1).start()

    def left_step(i, carry):
        c = tile_of(i)
        outer = lax.dot_general(g[my_rows], g[c, :], (((1,), (1,)), ((), ())), preferred_element_type=F32)
        left_v[:, c] = 0.95 * left_v[:, c] + 0.05 * outer
        return carry

    lax.fori_loop(0, size // width, left_step, 0)
    stores[2].start()

    pass_half()
    for k in range(1, n):
        norm_to(k).wait_recv()
    sums = stats[0]
    for i in range(1, n):
        sums = sums + stats[i]
    scale = jnp.sqrt(sums[0:1]) / (jnp.sqrt(sums[1:2]) + 1e-06)
    scales[own] = jnp.broadcast_to(scale, scales.shape[1:])

    def scale_to(k):
        return remote(scales.at[own], scales.at[own], ts.at[k], tr.at[k], "own", (own + k) % owners)

    for k in range(1, owners):
        scale_to(k).start()

    for cut in range(cuts):
        for k in range(1, pairs):
            to_pair(k, cut).wait_recv()
            to_core(k, cut).start()

    aligned = pl.ds(pl.multiple_of(group * LANES, LANES), LANES)

    def turn_step(i, carry):
        r = pl.ds(pl.multiple_of(i * LANES, LANES), LANES)
        turned[:, r] = g[r, aligned].T
        return carry

    lax.fori_loop(0, groups, turn_step, 0)
    offset = pl.ds(pl.multiple_of(me * rows - group * LANES, 8), rows)

    def right_step(i, carry):
        c = tile_of(i)
        product[...] = jnp.dot(turned[...], g[:, c], preferred_element_type=F32)
        right_v[:, c] = 0.95 * right_v[:, c] + 0.05 * product[offset]
        return carry

    lax.fori_loop(0, size // width, right_step, 0)
    stores[3].start()

    for k in range(1, owners):
        scale_to(k).wait_recv()
    for cut in range(cuts):
        for k in range(pairs):
            to_core(k, cut).wait_recv()
    for b in range(owners):
        factor = scales[owner[b]][0:1, 0:1]
        for column in range(2):
            scaled = (parts[owner[b], column].astype(F32) * factor).astype(BF16)
            if rows % LANES:
                scaled_v[b, :, pl.ds(column * (size // 2), size // 2)] = scaled
                continue
            for t in range(depth_z):
                scaled_v[b, :, pl.ds((2 * t + column) * rows, rows)] = scaled[:, t * rows:(t + 1) * rows]
        stores.append(pltpu.make_async_copy(scaled_v.at[b], direction.at[b], store_sem.at[4 + b]))
        stores[-1].start()

    for i, (s, h) in enumerate(steps):
        send_x(i).wait_send()
        gat_x(s, h).wait_send()
    for t in range(depth_z):
        for h in range(halves):
            @pl.when(z < t)
            def _():
                send_up(t, h).wait_send()

            @pl.when(z > t)
            def _():
                send_down(t, h).wait_send()

            @pl.when((z >= t) & has_above)
            def _():
                gat_up(t, h).wait_send()

            @pl.when((z <= t) & has_below)
            def _():
                gat_down(t, h).wait_send()
        @pl.when((z >= t) & has_above)
        def _():
            root_up(t).wait_send()

        @pl.when((z <= t) & has_below)
        def _():
            root_down(t).wait_send()
    root_x().wait_send()
    swap().wait_send()
    for k in range(1, n):
        norm_to(k).wait_send()
    for k in range(1, owners):
        scale_to(k).wait_send()
    for cut in range(cuts):
        for k in range(pairs):
            to_core(k, cut).wait_send()
            if k:
                to_pair(k, cut).wait_send()
    for copy in stores:
        copy.wait()


def finish_kernel(count, *refs):
    sources, targets, holds = refs[:count], refs[count:2 * count], refs[2 * count:3 * count]
    in_sem, out_sem = refs[3 * count:]
    copies = []
    for source, target, hold in zip(sources, targets, holds):
        blocks, rows, _ = source.shape
        cut = rows // 2 if blocks == 1 else rows
        for b in range(blocks):
            for at in range(0, rows, cut):
                piece = (b, pl.ds(at, cut))
                i = len(copies)
                copies.append((
                    pltpu.make_async_copy(source.at[piece], hold.at[piece], in_sem.at[i]),
                    pltpu.make_async_copy(hold.at[piece], target.at[piece], out_sem.at[i])))
    for load, _ in copies:
        load.start()
    for load, store in copies:
        load.wait()
        store.start()
    for _, store in copies:
        store.wait()


def finish(*arrays):
    count = len(arrays)
    pieces = sum(max(2, a.shape[0]) for a in arrays)
    anywhere = pl.BlockSpec(memory_space=pl.ANY)
    return pl.pallas_call(
        functools.partial(finish_kernel, count),
        out_shape=tuple(jax.ShapeDtypeStruct(a.shape, a.dtype) for a in arrays),
        in_specs=[anywhere] * count,
        out_specs=(anywhere,) * count,
        scratch_shapes=[pltpu.VMEM(a.shape, a.dtype) for a in arrays]
        + [pltpu.SemaphoreType.DMA((pieces,))] * 2,
        compiler_params=pltpu.CompilerParams(vmem_limit_bytes=VMEM),
    )(*arrays)


def body(n, owners, grads, left, right, root_left, root_right, first, second, owner):
    rows, size = left.shape[1:]
    line = n // 2
    halves = max(1, rows // 64)
    cuts = 2
    pairs = owners // 2
    sem = pltpu.SemaphoreType.DMA
    stat = jax.ShapeDtypeStruct((1, rows, size), F32)
    anywhere = pl.BlockSpec(memory_space=pl.ANY)
    hbm = pl.BlockSpec(memory_space=pltpu.HBM)
    *state, direction = pl.pallas_call(
        functools.partial(kernel, n, owners, halves, cuts),
        out_shape=(stat, stat, stat, stat, jax.ShapeDtypeStruct((owners, rows, size), BF16)),
        in_specs=[hbm] * 7 + [pl.BlockSpec(memory_space=pltpu.SMEM)],
        out_specs=(anywhere,) * 5,
        scratch_shapes=[
            *[pltpu.VMEM((line, rows, size), BF16)] * 4,
            pltpu.VMEM((rows, size), F32),
            pltpu.VMEM((size, size), BF16),
            pltpu.VMEM((size // 2, size), BF16),
            pltpu.VMEM((rows, size), F32),
            pltpu.VMEM((rows, size), F32),
            pltpu.VMEM((2 * rows, size), BF16),
            pltpu.VMEM((rows, size), F32),
            pltpu.VMEM((rows, size), F32),
            pltpu.VMEM((2 * rows, size), F32),
            pltpu.VMEM((LANES, size), BF16),
            pltpu.VMEM((LANES, 256), F32),
            pltpu.VMEM((owners, 2, rows, size // 2), BF16),
            pltpu.VMEM((owners, rows, size), BF16),
            pltpu.VMEM((rows, size // 2), BF16),
            pltpu.VMEM((8, LANES), F32),
            pltpu.VMEM((n, 8, LANES), F32),
            pltpu.VMEM((owners, 8, LANES), F32),
            sem((7,)), sem((4 + owners,)),
            sem((line * halves,)), sem((line * halves,)),
            *[sem((line, halves))] * 10,
            sem((1,)), sem((1,)),
            *[sem((line,))] * 4,
            sem((1,)), sem((1,)),
            *[sem((pairs, cuts))] * 4,
            sem((n,)), sem((n,)), sem((owners,)), sem((owners,)),
        ],
        compiler_params=pltpu.CompilerParams(
            collective_id=0, has_side_effects=True, vmem_limit_bytes=VMEM),
        cost_estimate=pl.CostEstimate(
            flops=8 * rows * size * size, bytes_accessed=24 * rows * size, transcendentals=rows * size),
    )(grads.reshape(line, 2, rows, size), left, right, root_left, root_right, first, second, owner)
    if rows % LANES:
        direction = direction.reshape(owners, rows, 2, line, rows).swapaxes(2, 3).reshape(owners, rows, size)
    return finish(*state, direction)


def solution(mesh):
    split = P("own", "dp", None)
    return jax.shard_map(
        functools.partial(body, mesh.shape["dp"], mesh.shape["own"]),
        mesh=mesh,
        in_specs=(P("dp", "own", None, None),) + (split,) * 6 + (P(),),
        out_specs=(split,) * 4 + (P(None, "dp", None),),
        check_vma=False,
    )
```
